128 devices in a mesh: row: 8 (over y, core), col: 16 (over x, z).
Axes of the slice: x: 4, y: 4, z: 4, core: 2. Of those that a mesh axis runs over, the one named last changes fastest.
Arguments:
- sigma_ss: bfloat16 [8192, 8192], P('col', 'row')
- l_cs: bfloat16 [6144, 8192], P('row', 'col'), may hold values from -4 to 4
- g_cc: bfloat16 [6144, 6144], P('row', 'col')
- pattern: int32 [16, 64], P(None, 'col'), may hold values 0 or 1
- sup_sizes: int32 [16], replicated, may hold values from 1 to 4, 48 in all
- owner: int32 [6144], P(('row', 'col')), may hold values from 0 to 6143, each once
Outputs:
- sel_cs: float32 [6144, 8192], P('row', 'col')
- log_var: float32 [6144], P(('row', 'col'))
The draws below stay inside these ranges and needn't reach their ends.
Inputs may be any that keep to these rules, and one draw needn't show every extreme that they name: `sup_sizes`: each child supernode holds between 1 and 4 blocks, and the sizes sum to 48. `owner`: each latent value of the child appears once.
All inputs are finite; a program needn't handle non-finite values. No bound on the sum of `pattern` on one device may be relied on, other than what follows from the above.
Results may differ from the reference program's by a relative error of at most 0.002.
The reference program's roundings to bfloat16 on the way (of `masked` and `zeta`) count: a program that leaves them out, or rounds other values in their place, can miss the bound.
Values may be sent and summed in bfloat16 or wider, within the bound.
A program may use at most 128 MiB of HBM per device.

```python
import math
import jax
import jax.numpy as jnp
import numpy as np
from jax import lax

NS = 8192
NC = 6144
BLK = 128
NSUP = 16


def draw_sigma_ss(key, part):
    key = jax.random.fold_in(key, 11)
    noise_key, diag_key, spread_key = jax.random.split(key, 3)
    noise = jax.random.normal(noise_key, (NS, NS), jnp.float32)
    diag_vals = jnp.exp(jax.random.uniform(diag_key, (NS,), jnp.float32, math.log(0.8), math.log(5.0)))
    spread = jax.random.uniform(spread_key, (NS,), jnp.float32, 0.7, 1.3)
    strength = 0.5
    reach = NS / 128.0
    places = jnp.arange(NS, dtype=jnp.int32).astype(jnp.float32)
    distance = jnp.abs(places[:, None] - places[None, :])
    kernel = strength * spread[:, None] * spread[None, :] * jnp.exp(-distance / reach)
    off_diag = (noise + noise.T) * (0.1 / math.sqrt(NS))
    indices = jnp.arange(NS, dtype=jnp.int32)
    on_diag = indices[:, None] == indices[None, :]
    whole = jnp.where(on_diag, diag_vals[:, None] + kernel, kernel + off_diag)
    return (whole * (1.0 / 64.0)).astype(jnp.bfloat16)


def draw_g_cc(key, part):
    key = jax.random.fold_in(key, 12)
    lower_key, diag_key, column_key = jax.random.split(key, 3)
    lower_vals = jax.random.normal(lower_key, (NC, NC), jnp.float32)
    diag_vals = jnp.exp(jax.random.uniform(diag_key, (NC,), jnp.float32, math.log(4.0), math.log(48.0)))
    column_scale = jnp.exp(jax.random.uniform(column_key, (NC,), jnp.float32, -1.0, 1.0))
    indices = jnp.arange(NC, dtype=jnp.int32)
    below = indices[:, None] > indices[None, :]
    on_diag = indices[:, None] == indices[None, :]
    scaled = lower_vals * column_scale[None, :] * (2.0 / math.sqrt(NC))
    return jnp.where(below, scaled, jnp.where(on_diag, diag_vals[:, None], 0.0)).astype(jnp.bfloat16)


def plant(array, stream_key, smallest, largest):
    place = [jax.random.randint(jax.random.fold_in(stream_key, axis), (), 0, length) for axis, length in enumerate(array.shape)]
    longest = array.shape.index(max(array.shape))
    neighbour = place[:longest] + [(place[longest] + 1) % array.shape[longest]] + place[longest + 1:]
    return array.at[tuple(place)].set(smallest).at[tuple(neighbour)].set(largest)


def steps_of(own_key, extent, pieces, least, high):
    def one(position, parts):
        draws = jax.random.uniform(jax.random.fold_in(jax.random.fold_in(own_key, 6), position), (parts,), jnp.float32, least / len(pieces), high / len(pieces))
        return jnp.repeat(jnp.exp(draws), extent[position] // parts).reshape((-1,) + (1,) * (len(extent) - position - 1))

    gain = one(*pieces[0])
    for cut in pieces[1:]:
        gain = gain * one(*cut)
    return gain


def length_profile(amount, total, most, skew):
    weights = [(1 << 20) // math.isqrt(standing ** skew) + 1 for standing in range(2, amount + 1)]
    surplus, holding = total - most - (amount - 1), [1] * (amount - 1)
    while surplus > 0:
        free = [i for i in range(amount - 1) if holding[i] < most]
        mass, left = sum([weights[i] for i in free]), surplus
        for i in free:
            addition = min(most - holding[i], max(1, left * weights[i] // mass), surplus)
            holding[i] = holding[i] + addition
            surplus = surplus - addition
    return np.array([most] + holding)


def uneven(key, amount, total, most, slope):
    if amount == 2:
        one = jax.random.randint(key, (), max(1, total - most), min(most, total - 1) + 1)
        return jnp.stack([one, total - one])
    tallies = jnp.asarray(length_profile(amount, total, most, slope), jnp.int32)
    couples = (amount - 1) // 2
    giver, sink = tallies[1:1 + 2 * couples:2], tallies[2:2 + 2 * couples:2]
    room = jnp.minimum(giver - 1, most - sink)
    moved = jax.random.randint(jax.random.fold_in(key, 1), (couples,), 0, 1 << 20) % (room + 1)
    tallies = tallies.at[1:1 + 2 * couples:2].set(giver - moved).at[2:2 + 2 * couples:2].set(sink + moved)
    return tallies[jax.random.permutation(jax.random.fold_in(key, 2), amount)]


def centred(own_key, shape, deviation, most, cuts=(), held_as=jnp.bfloat16):
    result = jax.random.normal(own_key, shape, jnp.float32) * deviation
    if len(cuts) > 0:
        result = steps_of(own_key, shape, cuts, -0.22, 0.18) * result
    return jnp.clip(result, min=-most, max=most).astype(held_as)


def setup_inputs(seed: int = 0) -> dict:
    splits = jax.random.split(jax.random.key(seed), 7)
    return {
        "sigma_ss": draw_sigma_ss(jax.random.fold_in(splits[6], 71), 0),
        "l_cs": centred(splits[1], (NC, NS), 0.3, 4.0, ((0, 8), (1, 16))),
        "g_cc": draw_g_cc(jax.random.fold_in(splits[6], 71), 0),
        "pattern": plant((jax.random.randint(splits[3], (NSUP, NS // BLK), 0, 3) < 1).astype(jnp.int32), jax.random.fold_in(splits[3], 1), 0, 1),
        "sup_sizes": uneven(splits[4], NSUP, NC // BLK, 4, 0).astype(jnp.int32),
        "owner": jax.random.permutation(splits[5], NC).astype(jnp.int32),
    }


def reference(sigma_ss, l_cs, g_cc, pattern, sup_sizes, owner):
    row_ends = (jnp.cumsum(sup_sizes) * BLK).astype(jnp.int32)
    child_rows = jnp.arange(NC, dtype=jnp.int32)
    supernode = jnp.sum((child_rows[:, None] >= row_ends[None, :]).astype(jnp.int32), axis=1)
    one_hot = (supernode[:, None] == jnp.arange(NSUP, dtype=jnp.int32)[None, :]).astype(jnp.float32)
    block_mask = jnp.dot(one_hot, pattern.astype(jnp.float32), precision=lax.Precision.HIGHEST)
    full_mask = jnp.repeat(block_mask, BLK, axis=1)
    masked = (l_cs.astype(jnp.float32) * full_mask).astype(jnp.bfloat16)
    zeta = jnp.dot(g_cc.T, masked, preferred_element_type=jnp.float32).astype(jnp.bfloat16)
    coupling = -jnp.dot(zeta, sigma_ss, preferred_element_type=jnp.float32)
    sel_cs = full_mask * coupling
    g_wide = g_cc.astype(jnp.float32)
    variance = jnp.sum(g_wide * g_wide, axis=0) - jnp.sum(coupling * zeta.astype(jnp.float32), axis=1)
    log_var = jnp.log(variance)[owner]
    return sel_cs, log_var
```

```python
import jax
import jax.numpy as jnp
from jax import lax
from jax.experimental import pallas as pl
from jax.experimental.pallas import tpu as pltpu
from jax.sharding import PartitionSpec as P

BLK = 128
NSUP = 16
MESH = pl.DeviceIdType.MESH
F32 = jnp.float32
BF16 = jnp.bfloat16
NQ = 4
FAR_ORDER = (2, 1, 3)


def kernel(
    gt_ref, masked_ref, sigma_ref, fac_ref,
    out_ref, fout_ref, cout_ref,
    gbuf, mbuf, sbuf, acc, far, near, zc, pbuf, rz, cross, fa, fb, ca, cb,
    local_sem, ga_send, ga_recv, gg_send, gg_recv,
    m_send, m_recv, m_sib_send, m_sib_recv,
    sa_send, sa_recv, s_send, s_recv, s_sib_send, s_sib_recv,
    y_send, y_recv, x_send, x_recv, z_send, z_recv,
    fr_send, fr_recv, fc_send, fc_recv, cr_send, cr_recv, cc_send, cc_recv,
):
    r = lax.axis_index("row")
    c = lax.axis_index("col")
    y, i = r // 2, r % 2
    x, z = c // 4, c % 4
    sib = 2 * y + 1 - i
    t = z // 2
    same = i == t
    other = i != t

    def at_x(d):
        return lax.rem(x + d, 4)

    def at_y(d):
        return lax.rem(y + d, 4)

    def at_z(d):
        return lax.rem(z + d, 4)

    def remote(src, dst, send, recv, row, col):
        return pltpu.make_async_remote_copy(
            src_ref=src, dst_ref=dst, send_sem=send, recv_sem=recv,
            device_id=(row, col), device_id_type=MESH,
        )

    def arrived(dst, recv):
        pltpu.make_async_copy(dst, dst, recv).wait()

    pending = []

    def send(*args):
        copy = remote(*args)
        copy.start()
        pending.append(copy)

    barrier = pltpu.get_barrier_semaphore()
    partners = [(r, lax.rem(c + d, 16)) for d in range(1, 16)]
    partners += [(lax.rem(r + d, 8), c) for d in range(1, 8)]
    partners += [(sib, 4 * at_x(d) + z) for d in range(1, 4)]
    partners += [(sib, 4 * x + at_z(d)) for d in range(1, 4)]
    for partner in partners:
        pl.semaphore_signal(barrier, inc=1, device_id=partner, device_id_type=MESH)
    pl.semaphore_wait(barrier, len(partners))

    def factor_dst():
        return gbuf.at[lax.rem(z, 2), x, i]

    def factor_copies(rel):
        copies = []
        for d in range(0 if rel else 1, 4):
            copies.append(remote(
                gt_ref.at[at_x(d)], factor_dst(), ga_send.at[d], ga_recv.at[d, rel],
                2 * y + t, 4 * at_x(d) + z,
            ))
        return copies

    @pl.when(same)
    def _():
        pltpu.make_async_copy(gt_ref.at[x], factor_dst(), local_sem.at[0]).start()
        for copy in factor_copies(0):
            copy.start()

    @pl.when(other)
    def _():
        for copy in factor_copies(1):
            copy.start()

    def sigma_copy(l):
        return remote(
            sigma_ref.at[l], sbuf.at[y, z],
            sa_send.at[l], sa_recv.at[lax.rem(z, 2)], 2 * y + t, 4 * x + 2 * i + l,
        )

    def sigma_own():
        return pltpu.make_async_copy(sigma_ref.at[lax.rem(z, 2)], sbuf.at[y, z], local_sem.at[1])

    def sigma_other():
        l = 1 - lax.rem(z, 2)
        return remote(
            sigma_ref.at[l], sbuf.at[y, z],
            sa_send.at[l], sa_recv.at[lax.rem(z, 2)], 2 * y + t, 4 * x + 2 * i + l,
        )

    @pl.when(same)
    def _():
        sigma_own().start()
        sigma_other().start()

    @pl.when(other)
    def _():
        sigma_copy(0).start()
        sigma_copy(1).start()

    def ring_first(src, slot, snd, rcv, right, left, me):
        send(src(0), slot(me, 0), snd.at[0], rcv.at[0], *right)
        send(src(1), slot(me, 1), snd.at[2], rcv.at[2], *left)
        send(src(1), slot(me, 1), snd.at[1], rcv.at[1], *right)
        send(src(0), slot(me, 0), snd.at[3], rcv.at[3], *left)

    def ring_forward(slot, snd, rcv, right, left, at):
        arrived(slot(at(3), 0), rcv.at[0])
        send(slot(at(3), 0), slot(at(3), 0), snd.at[4], rcv.at[4], *right)
        arrived(slot(at(1), 1), rcv.at[2])
        send(slot(at(1), 1), slot(at(1), 1), snd.at[5], rcv.at[5], *left)

    def ring_rest(slot, rcv, at):
        arrived(slot(at(3), 1), rcv.at[1])
        arrived(slot(at(1), 0), rcv.at[3])

    def ring_far(slot, rcv, at):
        arrived(slot(at(2), 0), rcv.at[4])
        arrived(slot(at(2), 1), rcv.at[5])

    x_right, x_left = (r, 4 * at_x(1) + z), (r, 4 * at_x(3) + z)
    y_right, y_left = (2 * at_y(1) + i, c), (2 * at_y(3) + i, c)

    def m_slot(place, half):
        return mbuf.at[i, place, half]

    def m_share(n, place):
        send(mbuf.at[i, place], mbuf.at[i, place], m_sib_send.at[n], m_sib_recv.at[n], sib, c)

    def s_slot(place, half):
        return sbuf.at[place, 2 * i + half]

    def s_share(n, place):
        block = sbuf.at[place, pl.ds(2 * i, 2)]
        send(block, block, s_sib_send.at[n], s_sib_recv.at[n], sib, c)

    ring_first(lambda h: masked_ref.at[h], m_slot, m_send, m_recv, x_right, x_left, x)
    send(masked_ref, mbuf.at[i, x], m_sib_send.at[0], m_sib_recv.at[0], sib, c)
    own_masked = pltpu.make_async_copy(masked_ref, mbuf.at[i, x], local_sem.at[2])
    own_masked.start()

    fa[r] = fac_ref[...]
    for d in range(1, 8):
        send(fac_ref, fa.at[r], fr_send.at[d], fr_recv.at[d], lax.rem(r + d, 8), c)

    @pl.when(same)
    def _():
        sigma_own().wait()
        m = 1 - lax.rem(z, 2)
        arrived(sbuf.at[y, 2 * i + m], sa_recv.at[m])

    @pl.when(other)
    def _():
        arrived(sbuf.at[y, 2 * i], sa_recv.at[0])
        arrived(sbuf.at[y, 2 * i + 1], sa_recv.at[1])

    ring_first(lambda h: s_slot(y, h), s_slot, s_send, s_recv, y_right, y_left, y)
    s_share(0, y)

    def spread_copies():
        slot = gbuf.at[lax.rem(z, 2)]
        return [
            remote(slot, slot, gg_send.at[d], gg_recv.at[lax.rem(z, 2)], r, 4 * x + at_z(d))
            for d in FAR_ORDER
        ]

    @pl.when(same)
    def _():
        pltpu.make_async_copy(gt_ref.at[x], factor_dst(), local_sem.at[0]).wait()
        for d in range(4):
            for rel in range(2):
                if d or rel:
                    src_core = 1 - i if rel else i
                    arrived(gbuf.at[lax.rem(z, 2), at_x(4 - d), src_core], ga_recv.at[d, rel])
        for copy in spread_copies():
            copy.start()

    ring_forward(m_slot, m_send, m_recv, x_right, x_left, at_x)
    ring_rest(m_slot, m_recv, at_x)
    m_share(1, at_x(3))
    m_share(2, at_x(1))
    ring_forward(s_slot, s_send, s_recv, y_right, y_left, at_y)
    ring_rest(s_slot, s_recv, at_y)
    s_share(1, at_y(3))
    s_share(2, at_y(1))

    for d in range(1, 8):
        arrived(fa.at[lax.rem(r + 8 - d, 8)], fr_recv.at[d])
    fb[c] = jnp.sum(fa[...], axis=0)
    for d in range(1, 16):
        send(fb.at[c], fb.at[c], fc_send.at[d], fc_recv.at[d], r, lax.rem(c + d, 16))

    ring_far(m_slot, m_recv, at_x)
    m_share(3, at_x(2))
    own_masked.wait()
    for zl in range(2):
        @pl.when(z != 2 * i + zl)
        def _():
            arrived(gbuf.at[zl], gg_recv.at[zl])
    for n, d in enumerate((0, 3, 1, 2)):
        arrived(mbuf.at[1 - i, at_x(d)], m_sib_recv.at[n])

    def zeta_part(q):
        zl, half = q // 2, q % 2
        g0 = gbuf[zl, :, 0, half].reshape(192, 768)
        g1 = gbuf[zl, :, 1, half].reshape(192, 768)

        def step(k, carry):
            total = jnp.dot(g0, mbuf[0, k].reshape(768, 512), preferred_element_type=F32)
            total += jnp.dot(g1, mbuf[1, k].reshape(768, 512), preferred_element_type=F32)
            acc[q, :, k] = total.reshape(4, 48, 512)
            return carry

        lax.fori_loop(0, 4, step, 0)

    low, high = pl.ds(0, 2), pl.ds(2, 2)

    def y_far(q):
        send(acc.at[q, at_y(2), low], far.at[q, 0], y_send.at[q, 0], y_recv.at[q, 0], *y_right)
        send(acc.at[q, at_y(2), high], far.at[q, 1], y_send.at[q, 1], y_recv.at[q, 1], *y_left)

    def y_direct(q):
        send(acc.at[q, at_y(1), high], near.at[q, 0, high], y_send.at[q, 2], y_recv.at[q, 2], *y_right)
        send(acc.at[q, at_y(3), low], near.at[q, 1, low], y_send.at[q, 3], y_recv.at[q, 3], *y_left)

    def y_combined(q):
        arrived(far.at[q, 0], y_recv.at[q, 0])
        acc[q, at_y(1), 0:2] += far[q, 0]
        send(acc.at[q, at_y(1), low], near.at[q, 0, low], y_send.at[q, 4], y_recv.at[q, 4], *y_right)
        arrived(far.at[q, 1], y_recv.at[q, 1])
        acc[q, at_y(3), 2:4] += far[q, 1]
        send(acc.at[q, at_y(3), high], near.at[q, 1, high], y_send.at[q, 5], y_recv.at[q, 5], *y_left)

    def zeta_done(q):
        arrived(near.at[q, 0, high], y_recv.at[q, 2])
        arrived(near.at[q, 1, low], y_recv.at[q, 3])
        arrived(near.at[q, 0, low], y_recv.at[q, 4])
        arrived(near.at[q, 1, high], y_recv.at[q, 5])
        zc[q, :, x] = (acc[q, y] + near[q, 0] + near[q, 1]).astype(BF16)
        for d in FAR_ORDER:
            send(zc.at[q, :, x], zc.at[q, :, x], x_send.at[q, d - 1], x_recv.at[q, d - 1], r, 4 * at_x(d) + z)

    def product(q, zt):
        total = None
        for k in range(4):
            part = lax.dot_general(
                zc[q, k].reshape(192, 512), sbuf[k, zt],
                (((1,), (1,)), ((), ())), preferred_element_type=F32,
            )
            total = part if total is None else total + part
        return total

    def coupling_part(q):
        for d in range(1, 4):
            arrived(zc.at[q, :, at_x(4 - d)], x_recv.at[q, d - 1])
        for d in FAR_ORDER:
            pbuf[q, d - 1] = product(q, at_z(d)).astype(BF16)
            send(pbuf.at[q, d - 1], rz.at[q, d - 1], z_send.at[q, d - 1], z_recv.at[q, d - 1], r, 4 * x + at_z(d))
        out_ref[q // 2, :, q % 2] = product(q, z).reshape(4, 48, 512)

    def coupling_done(q):
        zl, half = q // 2, q % 2
        for d in range(3):
            arrived(rz.at[q, d], z_recv.at[q, d])
        total = out_ref[zl, :, half].reshape(192, 512)
        total += rz[q, 0].astype(F32) + rz[q, 1].astype(F32) + rz[q, 2].astype(F32)
        total = -total
        out_ref[zl, :, half] = total.reshape(4, 48, 512)
        terms = total * zc[q, x].reshape(192, 512).astype(F32)
        terms = terms[:, 0:128] + terms[:, 128:256] + terms[:, 256:384] + terms[:, 384:512]
        cross[zl, :, half] = terms.reshape(4, 48, 128)

    zeta_part(0)
    y_far(0)
    y_direct(0)
    zeta_part(1)
    y_far(1)
    ring_far(s_slot, s_recv, at_y)
    s_share(3, at_y(2))
    y_combined(0)
    y_direct(1)
    zeta_part(2)
    y_far(2)
    y_combined(1)
    y_direct(2)
    zeta_part(3)
    zeta_done(0)
    y_far(3)
    y_combined(2)
    y_direct(3)
    for n, d in enumerate((0, 3, 1, 2)):
        arrived(sbuf.at[at_y(d), pl.ds(2 * (1 - i), 2)], s_sib_recv.at[n])
    for d in range(1, 16):
        arrived(fb.at[lax.rem(c + 16 - d, 16)], fc_recv.at[d])
    fout_ref[...] = fb[...]
    coupling_part(0)
    zeta_done(1)
    y_combined(3)
    coupling_part(1)
    coupling_done(0)
    zeta_done(2)
    coupling_part(2)
    coupling_done(1)
    zeta_done(3)
    coupling_done(2)
    coupling_part(3)
    coupling_done(3)

    sums = jnp.sum(cross[...].reshape(768, 128).T, axis=0, keepdims=True)
    ca[c] = jnp.zeros((8, 128), F32)
    for n in range(6):
        ca[c, n:n + 1] = sums[:, n * 128:(n + 1) * 128]
    for d in range(1, 16):
        send(ca.at[c], ca.at[c], cc_send.at[d], cc_recv.at[d], r, lax.rem(c + d, 16))
    for d in range(1, 16):
        arrived(ca.at[lax.rem(c + 16 - d, 16)], cc_recv.at[d])
    cb[r] = jnp.sum(ca[...], axis=0)
    for d in range(1, 8):
        send(cb.at[r], cb.at[r], cr_send.at[d], cr_recv.at[d], lax.rem(r + d, 8), c)
    for d in range(1, 8):
        arrived(cb.at[lax.rem(r + 8 - d, 8)], cr_recv.at[d])
    cout_ref[...] = cb[...]

    @pl.when(same)
    def _():
        for copy in factor_copies(0) + [sigma_other()] + spread_copies():
            copy.wait_send()

    @pl.when(other)
    def _():
        for copy in factor_copies(1) + [sigma_copy(0), sigma_copy(1)]:
            copy.wait_send()

    for copy in pending:
        copy.wait_send()


def selected_inverse(gt, masked, sigma, fac):
    dma = pltpu.SemaphoreType.DMA
    any_space = pl.BlockSpec(memory_space=pl.ANY)
    vmem = pl.BlockSpec(memory_space=pltpu.VMEM)
    return pl.pallas_call(
        kernel,
        out_shape=(
            jax.ShapeDtypeStruct((2, 4, 2, 48, 512), F32),
            jax.ShapeDtypeStruct((16, 8, 128), F32),
            jax.ShapeDtypeStruct((8, 8, 128), F32),
        ),
        in_specs=[any_space, any_space, any_space, vmem],
        out_specs=(vmem, vmem, vmem),
        scratch_shapes=[
            pltpu.VMEM((2, 4, 2, 2, 48, 768), BF16),
            pltpu.VMEM((2, 4, 2, 384, 512), BF16),
            pltpu.VMEM((4, 4, 512, 512), BF16),
            pltpu.VMEM((NQ, 4, 4, 48, 512), F32),
            pltpu.VMEM((NQ, 2, 2, 48, 512), F32),
            pltpu.VMEM((NQ, 2, 4, 48, 512), F32),
            pltpu.VMEM((NQ, 4, 4, 48, 512), BF16),
            pltpu.VMEM((NQ, 3, 192, 512), BF16),
            pltpu.VMEM((NQ, 3, 192, 512), BF16),
            pltpu.VMEM((2, 4, 2, 48, 128), F32),
            pltpu.VMEM((8, 8, 128), F32),
            pltpu.VMEM((16, 8, 128), F32),
            pltpu.VMEM((16, 8, 128), F32),
            pltpu.VMEM((8, 8, 128), F32),
            dma((3,)),
            dma((4,)), dma((4, 2)), dma((4,)), dma((2,)),
            dma((6,)), dma((6,)), dma((4,)), dma((4,)),
            dma((2,)), dma((2,)), dma((6,)), dma((6,)), dma((4,)), dma((4,)),
            dma((NQ, 6)), dma((NQ, 6)), dma((NQ, 3)), dma((NQ, 3)), dma((NQ, 3)), dma((NQ, 3)),
            dma((8,)), dma((8,)), dma((16,)), dma((16,)),
            dma((8,)), dma((8,)), dma((16,)), dma((16,)),
        ],
        compiler_params=pltpu.CompilerParams(
            collective_id=0, has_side_effects=True, vmem_limit_bytes=60 * 1024 * 1024
        ),
    )(gt, masked, sigma, fac)


def per_device(sigma_ss, l_cs, g_cc, pattern, sup_sizes, owner):
    local_rows = l_cs.shape[0]
    row_start = lax.axis_index("row") * local_rows
    row_ends = jnp.cumsum(sup_sizes) * BLK
    child_rows = row_start + jnp.arange(local_rows, dtype=jnp.int32)
    supernode = jnp.sum((child_rows[:, None] >= row_ends[None, :]).astype(jnp.int32), axis=1)
    one_hot = (supernode[:, None] == jnp.arange(NSUP, dtype=jnp.int32)[None, :]).astype(F32)
    block_mask = jnp.dot(one_hot, pattern.astype(F32), precision=lax.Precision.HIGHEST)
    full_mask = jnp.repeat(block_mask, BLK, axis=1)
    masked = (l_cs.astype(F32) * full_mask).astype(BF16)
    g_wide = g_cc.astype(F32)
    fac = jnp.sum(g_wide * g_wide, axis=0).reshape(3, 128)
    fac = jnp.concatenate([fac, jnp.zeros((5, 128), F32)], axis=0)
    gt = g_cc.T.reshape(4, 2, 48, 768)
    sigma = sigma_ss.reshape(512, 2, 512).transpose(1, 0, 2)
    coupling, factor_sums, cross_sums = selected_inverse(gt, masked.reshape(2, 384, 512), sigma, fac)
    sel_cs = full_mask * coupling.reshape(768, 512)
    variance = factor_sums[:, :3].reshape(6144) - cross_sums[:, :6].reshape(6144)
    log_all = jnp.log(variance)
    positions = jnp.arange(6144, dtype=jnp.int32)
    log_var = jnp.sum(
        jnp.where(owner[:, None] == positions[None, :], log_all[None, :], 0.0), axis=1
    )
    return (sel_cs, log_var)


def solution(mesh):
    in_specs = (
        P("col", "row"),
        P("row", "col"),
        P("row", "col"),
        P(None, "col"),
        P(),
        P(("row", "col")),
    )
    out_specs = (P("row", "col"), P(("row", "col")))
    return jax.shard_map(
        per_device, mesh=mesh, in_specs=in_specs, out_specs=out_specs, check_vma=False
    )
```

```python
import jax
import jax.numpy as jnp
from jax import lax
from jax.experimental import pallas as pl
from jax.experimental.pallas import tpu as pltpu
from jax.sharding import PartitionSpec as P

NSUP = 16
MESH = pl.DeviceIdType.MESH
F32 = jnp.float32
BF16 = jnp.bfloat16
NQ = 4
FAR_ORDER = (2, 1, 3)


def kernel(
    sigma_ref, l_ref, g_ref, pattern_ref, sizes_ref, owner_ref,
    out_ref, log_ref,
    gt_ref, gbuf, mbuf, sbuf, acc, ysend, yrecv, zc, pbuf, rz, cross, fac_ref, fa, ca, cb,
    local_sem, ga_send, ga_recv, gg_send, gg_recv,
    m_send, m_recv, m_sib_send, m_sib_recv,
    sa_send, sa_recv, s_send, s_recv, s_sib_send, s_sib_recv,
    y_send, y_recv, x_send, x_recv, z_send, z_recv,
    fr_send, fr_recv, cr_send, cr_recv, cc_send, cc_recv,
):
    r = lax.axis_index("row")
    c = lax.axis_index("col")
    y, i = r // 2, r % 2
    x, z = c // 4, c % 4
    sib = 2 * y + 1 - i
    t = z // 2
    same = i == t
    other = i != t

    def at_x(d):
        return lax.rem(x + d, 4)

    def at_y(d):
        return lax.rem(y + d, 4)

    def at_z(d):
        return lax.rem(z + d, 4)

    def remote(src, dst, send, recv, row, col):
        return pltpu.make_async_remote_copy(
            src_ref=src, dst_ref=dst, send_sem=send, recv_sem=recv,
            device_id=(row, col), device_id_type=MESH,
        )

    def arrived(dst, recv):
        pltpu.make_async_copy(dst, dst, recv).wait()

    pending = []

    def send(*args):
        copy = remote(*args)
        copy.start()
        pending.append(copy)

    barrier = pltpu.get_barrier_semaphore()
    partners = [(r, lax.rem(c + d, 16)) for d in range(1, 16)]
    partners += [(lax.rem(r + d, 8), c) for d in range(1, 8)]
    partners += [(sib, 4 * at_x(d) + z) for d in range(1, 4)]
    partners += [(sib, 4 * x + at_z(d)) for d in range(1, 4)]
    for partner in partners:
        pl.semaphore_signal(barrier, inc=1, device_id=partner, device_id_type=MESH)

    ends, total_size = [], jnp.int32(0)
    for s in range(NSUP):
        total_size = total_size + sizes_ref[s]
        ends.append(total_size)
    block_mask = []
    for n in range(6):
        place = jnp.int32(0)
        for s in range(NSUP):
            place = place + (ends[s] <= 6 * r + n).astype(jnp.int32)
        place = jnp.minimum(place, NSUP - 1)
        block_mask.append([pattern_ref[place, m].astype(F32) for m in range(4)])

    gt_ref[...] = g_ref[...].T.reshape(4, 2, 48, 768)
    wide = g_ref[...].astype(F32)
    squares = jnp.sum(wide * wide, axis=0, keepdims=True)
    fac_ref[...] = jnp.zeros((8, 128), F32)
    for n in range(3):
        fac_ref[n:n + 1] = squares[:, n * 128:(n + 1) * 128]

    pl.semaphore_wait(barrier, len(partners))

    fa[r] = fac_ref[...]
    for d in range(1, 8):
        send(fac_ref, fa.at[r], fr_send.at[d], fr_recv.at[d], lax.rem(r + d, 8), c)

    def factor_dst():
        return gbuf.at[lax.rem(z, 2), x, i]

    def factor_copies(rel):
        copies = []
        for d in range(0 if rel else 1, 4):
            copies.append(remote(
                gt_ref.at[at_x(d)], factor_dst(), ga_send.at[d], ga_recv.at[d, rel],
                2 * y + t, 4 * at_x(d) + z,
            ))
        return copies

    @pl.when(same)
    def _():
        pltpu.make_async_copy(gt_ref.at[x], factor_dst(), local_sem.at[0]).start()
        for copy in factor_copies(0):
            copy.start()

    @pl.when(other)
    def _():
        for copy in factor_copies(1):
            copy.start()

    def sigma_copy(l):
        return remote(
            sigma_ref.at[:, pl.ds(l * 512, 512)], sbuf.at[y, z],
            sa_send.at[l], sa_recv.at[lax.rem(z, 2)], 2 * y + t, 4 * x + 2 * i + l,
        )

    def sigma_own():
        return pltpu.make_async_copy(sigma_ref.at[:, pl.ds(pl.multiple_of(lax.rem(z, 2) * 512, 512), 512)], sbuf.at[y, z], local_sem.at[1])

    def sigma_other():
        l = 1 - lax.rem(z, 2)
        return remote(
            sigma_ref.at[:, pl.ds(pl.multiple_of(l * 512, 512), 512)], sbuf.at[y, z],
            sa_send.at[l], sa_recv.at[lax.rem(z, 2)], 2 * y + t, 4 * x + 2 * i + l,
        )

    @pl.when(same)
    def _():
        sigma_own().start()
        sigma_other().start()

    @pl.when(other)
    def _():
        sigma_copy(0).start()
        sigma_copy(1).start()

    def ring_first(src, slot, snd, rcv, right, left, me):
        send(src(0), slot(me, 0), snd.at[0], rcv.at[0], *right)
        send(src(1), slot(me, 1), snd.at[2], rcv.at[2], *left)
        send(src(1), slot(me, 1), snd.at[1], rcv.at[1], *right)
        send(src(0), slot(me, 0), snd.at[3], rcv.at[3], *left)

    def ring_forward(slot, snd, rcv, right, left, at):
        arrived(slot(at(3), 0), rcv.at[0])
        send(slot(at(3), 0), slot(at(3), 0), snd.at[4], rcv.at[4], *right)
        arrived(slot(at(1), 1), rcv.at[2])
        send(slot(at(1), 1), slot(at(1), 1), snd.at[5], rcv.at[5], *left)

    def ring_rest(slot, rcv, at):
        arrived(slot(at(3), 1), rcv.at[1])
        arrived(slot(at(1), 0), rcv.at[3])

    def ring_far(slot, rcv, at):
        arrived(slot(at(2), 0), rcv.at[4])
        arrived(slot(at(2), 1), rcv.at[5])

    x_right, x_left = (r, 4 * at_x(1) + z), (r, 4 * at_x(3) + z)
    y_right, y_left = (2 * at_y(1) + i, c), (2 * at_y(3) + i, c)

    def m_slot(place, half):
        return mbuf.at[i, place, half]

    def m_share(n, place):
        send(mbuf.at[i, place], mbuf.at[i, place], m_sib_send.at[n], m_sib_recv.at[n], sib, c)

    def s_slot(place, half):
        return sbuf.at[place, 2 * i + half]

    def s_share(n, place):
        block = sbuf.at[place, pl.ds(2 * i, 2)]
        send(block, block, s_sib_send.at[n], s_sib_recv.at[n], sib, c)

    for n in range(6):
        for m in range(4):
            block = l_ref[n * 128:(n + 1) * 128, m * 128:(m + 1) * 128].astype(F32)
            mbuf[i, x, n // 3, (n % 3) * 128:(n % 3 + 1) * 128, m * 128:(m + 1) * 128] = (
                block * block_mask[n][m]
            ).astype(BF16)
    ring_first(lambda h: m_slot(x, h), m_slot, m_send, m_recv, x_right, x_left, x)
    m_share(0, x)
    @pl.when(same)
    def _():
        sigma_own().wait()
        m = 1 - lax.rem(z, 2)
        arrived(sbuf.at[y, 2 * i + m], sa_recv.at[m])

    @pl.when(other)
    def _():
        arrived(sbuf.at[y, 2 * i], sa_recv.at[0])
        arrived(sbuf.at[y, 2 * i + 1], sa_recv.at[1])

    ring_first(lambda h: s_slot(y, h), s_slot, s_send, s_recv, y_right, y_left, y)
    s_share(0, y)

    def spread_copies():
        slot = gbuf.at[lax.rem(z, 2)]
        return [
            remote(slot, slot, gg_send.at[d], gg_recv.at[lax.rem(z, 2)], r, 4 * x + at_z(d))
            for d in FAR_ORDER
        ]

    @pl.when(same)
    def _():
        pltpu.make_async_copy(gt_ref.at[x], factor_dst(), local_sem.at[0]).wait()
        for d in range(4):
            for rel in range(2):
                if d or rel:
                    src_core = 1 - i if rel else i
                    arrived(gbuf.at[lax.rem(z, 2), at_x(4 - d), src_core], ga_recv.at[d, rel])
        for copy in spread_copies():
            copy.start()

    ring_forward(m_slot, m_send, m_recv, x_right, x_left, at_x)
    ring_rest(m_slot, m_recv, at_x)
    m_share(1, at_x(3))
    m_share(2, at_x(1))
    ring_forward(s_slot, s_send, s_recv, y_right, y_left, at_y)
    ring_rest(s_slot, s_recv, at_y)
    s_share(1, at_y(3))
    s_share(2, at_y(1))

    ring_far(m_slot, m_recv, at_x)
    m_share(3, at_x(2))
    for zl in range(2):
        @pl.when(z != 2 * i + zl)
        def _():
            arrived(gbuf.at[zl], gg_recv.at[zl])
    for n, d in enumerate((0, 3, 1, 2)):
        arrived(mbuf.at[1 - i, at_x(d)], m_sib_recv.at[n])

    def zeta_part(q):
        zl, half = q // 2, q % 2
        g0 = gbuf[zl, :, 0, half].reshape(192, 768)
        g1 = gbuf[zl, :, 1, half].reshape(192, 768)

        def step(k, carry):
            total = jnp.dot(g0, mbuf[0, k].reshape(768, 512), preferred_element_type=F32)
            total += jnp.dot(g1, mbuf[1, k].reshape(768, 512), preferred_element_type=F32)
            acc[q, :, k] = total.reshape(4, 48, 512)
            return carry

        lax.fori_loop(0, 4, step, 0)

    def zeta_send(q):
        for d in FAR_ORDER:
            parts = [acc[q, at_y(d), k] for k in range(4)]
            top = jnp.abs(parts[0])
            for part in parts[1:]:
                top = jnp.maximum(top, jnp.abs(part))
            top = jnp.max(top, axis=1, keepdims=True)
            power = jnp.floor(jnp.log2(jnp.maximum(top, 1e-30)) + 1.01)
            up = jnp.exp2(15.0 - power)
            for k in range(4):
                code = jnp.round(parts[k] * up).astype(jnp.int32).astype(jnp.int16)
                ysend[q, d - 1, :, k * 512:(k + 1) * 512] = code
            ysend[q, d - 1, :, 2048:] = jnp.broadcast_to(
                power.astype(jnp.int32), (48, 128)
            ).astype(jnp.int16)
            send(
                ysend.at[q, d - 1], yrecv.at[q, d - 1],
                y_send.at[q, d - 1], y_recv.at[q, d - 1], 2 * at_y(d) + i, c,
            )

    def zeta_done(q):
        for d in range(3):
            arrived(yrecv.at[q, d], y_recv.at[q, d])
        down = []
        for d in range(3):
            power = yrecv[q, d, :, 2048:].astype(jnp.int32).astype(F32)
            down.append(jnp.exp2(power - 15.0)[:, 0:1])
        for k in range(4):
            total = acc[q, y, k]
            for d in range(3):
                code = yrecv[q, d, :, k * 512:(k + 1) * 512]
                total += code.astype(jnp.int32).astype(F32) * down[d]
            zc[q, k, x] = total.astype(BF16)
        for d in FAR_ORDER:
            send(zc.at[q, :, x], zc.at[q, :, x], x_send.at[q, d - 1], x_recv.at[q, d - 1], r, 4 * at_x(d) + z)

    def product(q, zt):
        total = None
        for k in range(4):
            part = lax.dot_general(
                zc[q, k].reshape(192, 512), sbuf[k, zt],
                (((1,), (1,)), ((), ())), preferred_element_type=F32,
            )
            total = part if total is None else total + part
        return total

    def first_row(q, place):
        return (q // 2) * 384 + place * 96 + (q % 2) * 48

    def put_rows(q, total):
        for place in range(4):
            out_ref[pl.ds(first_row(q, place), 48), :] = total[place * 48:(place + 1) * 48]

    def coupling_part(q):
        for d in range(1, 4):
            arrived(zc.at[q, :, at_x(4 - d)], x_recv.at[q, d - 1])
        for d in FAR_ORDER:
            pbuf[q, d - 1] = product(q, at_z(d)).astype(BF16)
            send(pbuf.at[q, d - 1], rz.at[q, d - 1], z_send.at[q, d - 1], z_recv.at[q, d - 1], r, 4 * x + at_z(d))
        put_rows(q, product(q, z))

    def coupling_done(q):
        for d in range(3):
            arrived(rz.at[q, d], z_recv.at[q, d])
        total = jnp.concatenate(
            [out_ref[pl.ds(first_row(q, place), 48), :] for place in range(4)], axis=0
        )
        total += rz[q, 0].astype(F32) + rz[q, 1].astype(F32) + rz[q, 2].astype(F32)
        total = -total
        put_rows(q, total)
        terms = total * zc[q, x].reshape(192, 512).astype(F32)
        terms = terms[:, 0:128] + terms[:, 128:256] + terms[:, 256:384] + terms[:, 384:512]
        for place in range(4):
            cross[pl.ds(first_row(q, place), 48), :] = terms[place * 48:(place + 1) * 48]

    zeta_part(0)
    zeta_send(0)
    ring_far(s_slot, s_recv, at_y)
    s_share(3, at_y(2))
    zeta_part(1)
    zeta_send(1)
    zeta_done(0)
    zeta_part(2)
    zeta_send(2)
    zeta_done(1)
    zeta_part(3)
    zeta_send(3)
    for n, d in enumerate((0, 3, 1, 2)):
        arrived(sbuf.at[at_y(d), pl.ds(2 * (1 - i), 2)], s_sib_recv.at[n])
    coupling_part(0)
    zeta_done(2)
    coupling_part(1)
    coupling_done(0)
    zeta_done(3)
    coupling_part(2)
    coupling_done(1)
    for d in range(1, 8):
        arrived(fa.at[lax.rem(r + 8 - d, 8)], fr_recv.at[d])
    ca[c, 8:16] = jnp.sum(fa[...], axis=0)
    ca[c, 0:8] = jnp.zeros((8, 128), F32)
    coupling_part(3)
    coupling_done(2)
    coupling_done(3)

    sums = jnp.sum(cross[...].T, axis=0, keepdims=True)
    for n in range(6):
        ca[c, n:n + 1] = sums[:, n * 128:(n + 1) * 128]
    for d in range(1, 16):
        send(ca.at[c], ca.at[c], cc_send.at[d], cc_recv.at[d], r, lax.rem(c + d, 16))
    for n in range(6):
        for m in range(4):
            rows, columns = slice(n * 128, (n + 1) * 128), slice(m * 128, (m + 1) * 128)
            out_ref[rows, columns] = out_ref[rows, columns] * block_mask[n][m]
    for d in range(1, 16):
        arrived(ca.at[lax.rem(c + 16 - d, 16)], cc_recv.at[d])
    cb[r] = jnp.sum(ca[:, 0:8], axis=0)
    for d in range(1, 8):
        send(cb.at[r], cb.at[r], cr_send.at[d], cr_recv.at[d], lax.rem(r + d, 8), c)
    wanted = jnp.broadcast_to(owner_ref[...].astype(F32), (128, 48)).T
    lanes = lax.broadcasted_iota(jnp.int32, (48, 128), 1).astype(F32)
    for d in range(1, 8):
        arrived(cb.at[lax.rem(r + 8 - d, 8)], cr_recv.at[d])
    picked = jnp.zeros((48, 128), F32)
    for n in range(48):
        row = jnp.log(ca[n // 3, 8 + n % 3:9 + n % 3] - cb[n // 6, n % 6:n % 6 + 1])
        picked = jnp.where(wanted - float(128 * n) == lanes, row, picked)
    log_ref[...] = jnp.sum(picked.T, axis=0, keepdims=True)

    @pl.when(same)
    def _():
        for copy in factor_copies(0) + [sigma_other()] + spread_copies():
            copy.wait_send()

    @pl.when(other)
    def _():
        for copy in factor_copies(1) + [sigma_copy(0), sigma_copy(1)]:
            copy.wait_send()

    for copy in pending:
        copy.wait_send()


def per_device(sigma_ss, l_cs, g_cc, pattern, sup_sizes, owner):
    dma = pltpu.SemaphoreType.DMA
    any_space = pl.BlockSpec(memory_space=pl.ANY)
    vmem = pl.BlockSpec(memory_space=pltpu.VMEM)
    smem = pl.BlockSpec(memory_space=pltpu.SMEM)
    sel_cs, log_var = pl.pallas_call(
        kernel,
        out_shape=(
            jax.ShapeDtypeStruct((768, 512), F32),
            jax.ShapeDtypeStruct((1, 48), F32),
        ),
        in_specs=[any_space, vmem, vmem, smem, smem, vmem],
        out_specs=(vmem, vmem),
        scratch_shapes=[
            pltpu.VMEM((4, 2, 48, 768), BF16),
            pltpu.VMEM((2, 4, 2, 2, 48, 768), BF16),
            pltpu.VMEM((2, 4, 2, 384, 512), BF16),
            pltpu.VMEM((4, 4, 512, 512), BF16),
            pltpu.VMEM((NQ, 4, 4, 48, 512), F32),
            pltpu.VMEM((NQ, 3, 48, 2176), jnp.int16),
            pltpu.VMEM((NQ, 3, 48, 2176), jnp.int16),
            pltpu.VMEM((NQ, 4, 4, 48, 512), BF16),
            pltpu.VMEM((NQ, 3, 192, 512), BF16),
            pltpu.VMEM((NQ, 3, 192, 512), BF16),
            pltpu.VMEM((768, 128), F32),
            pltpu.VMEM((8, 128), F32),
            pltpu.VMEM((8, 8, 128), F32),
            pltpu.VMEM((16, 16, 128), F32),
            pltpu.VMEM((8, 8, 128), F32),
            dma((3,)),
            dma((4,)), dma((4, 2)), dma((4,)), dma((2,)),
            dma((6,)), dma((6,)), dma((4,)), dma((4,)),
            dma((2,)), dma((2,)), dma((6,)), dma((6,)), dma((4,)), dma((4,)),
            dma((NQ, 3)), dma((NQ, 3)), dma((NQ, 3)), dma((NQ, 3)), dma((NQ, 3)), dma((NQ, 3)),
            dma((8,)), dma((8,)),
            dma((8,)), dma((8,)), dma((16,)), dma((16,)),
        ],
        compiler_params=pltpu.CompilerParams(
            collective_id=0, has_side_effects=True, vmem_limit_bytes=60 * 1024 * 1024
        ),
    )(sigma_ss, l_cs, g_cc, pattern, sup_sizes, owner.reshape(1, 48))
    return (sel_cs, log_var.reshape(48))


def solution(mesh):
    in_specs = (
        P("col", "row"),
        P("row", "col"),
        P("row", "col"),
        P(None, "col"),
        P(),
        P(("row", "col")),
    )
    out_specs = (P("row", "col"), P(("row", "col")))
    return jax.shard_map(
        per_device, mesh=mesh, in_specs=in_specs, out_specs=out_specs, check_vma=False
    )
```

```python
import jax
import jax.numpy as jnp
from jax import lax
from jax.experimental import pallas as pl
from jax.experimental.pallas import tpu as pltpu
from jax.sharding import PartitionSpec as P

NSUP = 16
MESH = pl.DeviceIdType.MESH
F32 = jnp.float32
BF16 = jnp.bfloat16
CHUNKS = ((0, 0, 48), (0, 48, 48), (1, 0, 48), (1, 48, 32), (1, 80, 16))
NQ = len(CHUNKS)
FAR_ORDER = (2, 1, 3)


def kernel(
    sigma_ref, l_ref, g_ref, pattern_ref, sizes_ref, owner_ref,
    out_ref, log_ref,
    gt_ref, gbuf, mbuf, sbuf, acc, ysend, yrecv, zc, pbuf, rz, cross, fac_ref, fa, ca, cb,
    local_sem, ga_send, ga_recv, gg_send, gg_recv,
    m_send, m_recv, m_sib_send, m_sib_recv,
    sa_send, sa_recv, s_send, s_recv, s_sib_send, s_sib_recv,
    y_send, y_recv, x_send, x_recv, z_send, z_recv,
    fr_send, fr_recv, cr_send, cr_recv, cc_send, cc_recv,
):
    r = lax.axis_index("row")
    c = lax.axis_index("col")
    y, i = r // 2, r % 2
    x, z = c // 4, c % 4
    sib = 2 * y + 1 - i
    t = z // 2
    same = i == t
    other = i != t

    def at_x(d):
        return lax.rem(x + d, 4)

    def at_y(d):
        return lax.rem(y + d, 4)

    def at_z(d):
        return lax.rem(z + d, 4)

    def remote(src, dst, send, recv, row, col):
        return pltpu.make_async_remote_copy(
            src_ref=src, dst_ref=dst, send_sem=send, recv_sem=recv,
            device_id=(row, col), device_id_type=MESH,
        )

    def arrived(dst, recv):
        pltpu.make_async_copy(dst, dst, recv).wait()

    pending = []

    def send(*args):
        copy = remote(*args)
        copy.start()
        pending.append(copy)

    barrier = pltpu.get_barrier_semaphore()
    partners = [(r, lax.rem(c + d, 16)) for d in range(1, 16)]
    partners += [(lax.rem(r + d, 8), c) for d in range(1, 8)]
    partners += [(sib, 4 * at_x(d) + z) for d in range(1, 4)]
    partners += [(sib, 4 * x + at_z(d)) for d in range(1, 4)]
    for partner in partners:
        pl.semaphore_signal(barrier, inc=1, device_id=partner, device_id_type=MESH)

    ends, total_size = [], jnp.int32(0)
    for s in range(NSUP):
        total_size = total_size + sizes_ref[s]
        ends.append(total_size)
    block_mask = []
    for n in range(6):
        place = jnp.int32(0)
        for s in range(NSUP):
            place = place + (ends[s] <= 6 * r + n).astype(jnp.int32)
        place = jnp.minimum(place, NSUP - 1)
        row = pattern_ref[pl.ds(place, 1), :].astype(F32)
        block_mask.append([row[:, m:m + 1] for m in range(4)])

    for n in range(6):
        for m in range(4):
            block = l_ref[n * 128:(n + 1) * 128, m * 128:(m + 1) * 128].astype(F32)
            mbuf[i, x, n // 3, (n % 3) * 128:(n % 3 + 1) * 128, m * 128:(m + 1) * 128] = (
                block * block_mask[n][m]
            ).astype(BF16)
    gt_ref[...] = g_ref[...].T.reshape(4, 96, 768)
    wide = g_ref[...].astype(F32)
    squares = jnp.sum(wide * wide, axis=0, keepdims=True)
    fac_ref[...] = jnp.zeros((8, 128), F32)
    for n in range(3):
        fac_ref[n:n + 1] = squares[:, n * 128:(n + 1) * 128]

    pl.semaphore_wait(barrier, len(partners))

    fa[r] = fac_ref[...]
    for d in range(1, 8):
        send(fac_ref, fa.at[r], fr_send.at[d], fr_recv.at[d], lax.rem(r + d, 8), c)

    def factor_dst():
        return gbuf.at[lax.rem(z, 2), x, i]

    def factor_copies(rel):
        copies = []
        for d in range(0 if rel else 1, 4):
            copies.append(remote(
                gt_ref.at[at_x(d)], factor_dst(), ga_send.at[d], ga_recv.at[d, rel],
                2 * y + t, 4 * at_x(d) + z,
            ))
        return copies

    @pl.when(same)
    def _():
        pltpu.make_async_copy(gt_ref.at[x], factor_dst(), local_sem.at[0]).start()
        for copy in factor_copies(0):
            copy.start()

    @pl.when(other)
    def _():
        for copy in factor_copies(1):
            copy.start()

    def sigma_part(l, half):
        return sigma_ref.at[pl.ds(half * 256, 256), pl.ds(pl.multiple_of(l * 512, 512), 512)]

    def sigma_own():
        return [
            pltpu.make_async_copy(sigma_part(lax.rem(z, 2), h), sbuf.at[y, z, h], local_sem.at[1 + h])
            for h in range(2)
        ]

    def sigma_copy(l):
        return [
            remote(
                sigma_part(l, h), sbuf.at[y, z, h],
                sa_send.at[l, h], sa_recv.at[lax.rem(z, 2), h], 2 * y + t, 4 * x + 2 * i + l,
            )
            for h in range(2)
        ]

    @pl.when(same)
    def _():
        for copy in sigma_own() + sigma_copy(1 - lax.rem(z, 2)):
            copy.start()

    @pl.when(other)
    def _():
        for first, second in zip(sigma_copy(0), sigma_copy(1)):
            first.start()
            second.start()

    def ring_first(src, slot, snd, rcv, right, left, me):
        send(src(0), slot(me, 0), snd.at[0], rcv.at[0], *right)
        send(src(1), slot(me, 1), snd.at[2], rcv.at[2], *left)
        send(src(1), slot(me, 1), snd.at[1], rcv.at[1], *right)
        send(src(0), slot(me, 0), snd.at[3], rcv.at[3], *left)

    def ring_forward(slot, snd, rcv, right, left, at):
        arrived(slot(at(3), 0), rcv.at[0])
        send(slot(at(3), 0), slot(at(3), 0), snd.at[4], rcv.at[4], *right)
        arrived(slot(at(1), 1), rcv.at[2])
        send(slot(at(1), 1), slot(at(1), 1), snd.at[5], rcv.at[5], *left)

    def ring_rest(slot, rcv, at):
        arrived(slot(at(3), 1), rcv.at[1])
        arrived(slot(at(1), 0), rcv.at[3])

    def ring_far(slot, rcv, at):
        arrived(slot(at(2), 0), rcv.at[4])
        arrived(slot(at(2), 1), rcv.at[5])

    x_right, x_left = (r, 4 * at_x(1) + z), (r, 4 * at_x(3) + z)
    y_right, y_left = (2 * at_y(1) + i, c), (2 * at_y(3) + i, c)

    def m_slot(place, half):
        return mbuf.at[i, place, half]

    def m_share(n, place):
        send(mbuf.at[i, place], mbuf.at[i, place], m_sib_send.at[n], m_sib_recv.at[n], sib, c)

    s_block = [jnp.where(same, lax.rem(z, 2), 0)]
    s_block.append(1 - s_block[0])

    def s_slot(order):
        return lambda place, half: sbuf.at[place, 2 * i + s_block[order], half]

    def s_share(order, n, place):
        block = sbuf.at[place, 2 * i + s_block[order]]
        send(block, block, s_sib_send.at[order, n], s_sib_recv.at[order, n], sib, c)

    def s_first(order):
        slot = s_slot(order)
        snd, rcv = s_send.at[order], s_recv.at[order]
        ring_first(lambda h: slot(y, h), slot, snd, rcv, y_right, y_left, y)
        s_share(order, 0, y)

    def s_forward(order):
        ring_forward(s_slot(order), s_send.at[order], s_recv.at[order], y_right, y_left, at_y)

    def s_rest(order):
        ring_rest(s_slot(order), s_recv.at[order], at_y)
        s_share(order, 1, at_y(3))
        s_share(order, 2, at_y(1))

    def s_far(order):
        ring_far(s_slot(order), s_recv.at[order], at_y)
        s_share(order, 3, at_y(2))

    def s_all():
        for order in range(2):
            for n, d in enumerate((0, 3, 1, 2)):
                place = 2 * (1 - i) + sib_block[order]
                arrived(sbuf.at[at_y(d), place], s_sib_recv.at[order, n])

    sib_block = [jnp.where(other, lax.rem(z, 2), 0)]
    sib_block.append(1 - sib_block[0])

    ring_first(lambda h: m_slot(x, h), m_slot, m_send, m_recv, x_right, x_left, x)
    m_share(0, x)

    @pl.when(same)
    def _():
        for copy in sigma_own():
            copy.wait()

    @pl.when(other)
    def _():
        for h in range(2):
            arrived(sbuf.at[y, 2 * i, h], sa_recv.at[0, h])

    s_first(0)

    for h in range(2):
        arrived(sbuf.at[y, 2 * i + s_block[1], h], sa_recv.at[s_block[1], h])
    s_first(1)

    def spread_copies():
        slot = gbuf.at[lax.rem(z, 2)]
        return [
            remote(slot, slot, gg_send.at[d], gg_recv.at[lax.rem(z, 2)], r, 4 * x + at_z(d))
            for d in FAR_ORDER
        ]

    @pl.when(same)
    def _():
        pltpu.make_async_copy(gt_ref.at[x], factor_dst(), local_sem.at[0]).wait()
        for d in range(4):
            for rel in range(2):
                if d or rel:
                    src_core = 1 - i if rel else i
                    arrived(gbuf.at[lax.rem(z, 2), at_x(4 - d), src_core], ga_recv.at[d, rel])
        for copy in spread_copies():
            copy.start()

    s_forward(0)
    ring_forward(m_slot, m_send, m_recv, x_right, x_left, at_x)
    ring_rest(m_slot, m_recv, at_x)
    m_share(1, at_x(3))
    m_share(2, at_x(1))
    s_rest(0)
    s_forward(1)
    s_rest(1)

    ring_far(m_slot, m_recv, at_x)
    m_share(3, at_x(2))
    for zl in range(2):
        @pl.when(z != 2 * i + zl)
        def _():
            arrived(gbuf.at[zl], gg_recv.at[zl])
    for n, d in enumerate((0, 3, 1, 2)):
        arrived(mbuf.at[1 - i, at_x(d)], m_sib_recv.at[n])

    def zeta_part(q):
        zl, start, rows = CHUNKS[q]
        here = slice(start, start + rows)
        g0 = gbuf[zl, :, 0, here].reshape(4 * rows, 768)
        g1 = gbuf[zl, :, 1, here].reshape(4 * rows, 768)

        def step(k, carry):
            total = jnp.dot(g0, mbuf[0, k].reshape(768, 512), preferred_element_type=F32)
            total += jnp.dot(g1, mbuf[1, k].reshape(768, 512), preferred_element_type=F32)
            acc[zl, :, k, here] = total.reshape(4, rows, 512)
            return carry

        lax.fori_loop(0, 4, step, 0)

    def zeta_send(q):
        zl, start, rows = CHUNKS[q]
        here = slice(start, start + rows)
        for d in FAR_ORDER:
            parts = [acc[zl, at_y(d), k, here] for k in range(4)]
            top = jnp.abs(parts[0])
            for part in parts[1:]:
                top = jnp.maximum(top, jnp.abs(part))
            top = jnp.max(top, axis=1, keepdims=True)
            power = jnp.floor(jnp.log2(jnp.maximum(top, 1e-30)) + 1.01)
            up = jnp.exp2(15.0 - power)
            for k in range(4):
                code = jnp.round(parts[k] * up).astype(jnp.int32).astype(jnp.int16)
                ysend[zl, d - 1, here, k * 512:(k + 1) * 512] = code
            ysend[zl, d - 1, here, 2048:] = jnp.broadcast_to(
                power.astype(jnp.int32), (rows, 128)
            ).astype(jnp.int16)
            send(
                ysend.at[zl, d - 1, pl.ds(start, rows)], yrecv.at[zl, d - 1, pl.ds(start, rows)],
                y_send.at[q, d - 1], y_recv.at[q, d - 1], 2 * at_y(d) + i, c,
            )

    def zeta_done(q):
        zl, start, rows = CHUNKS[q]
        here = slice(start, start + rows)
        for d in range(3):
            arrived(yrecv.at[zl, d, pl.ds(start, rows)], y_recv.at[q, d])
        down = []
        for d in range(3):
            power = yrecv[zl, d, here, 2048:].astype(jnp.int32).astype(F32)
            down.append(jnp.exp2(power - 15.0)[:, 0:1])
        for k in range(4):
            total = acc[zl, y, k, here]
            for d in range(3):
                code = yrecv[zl, d, here, k * 512:(k + 1) * 512]
                total += code.astype(jnp.int32).astype(F32) * down[d]
            zc[zl, k, x, here] = total.astype(BF16)
        block = zc.at[zl, :, x, pl.ds(start, rows)]
        for d in FAR_ORDER:
            send(block, block, x_send.at[q, d - 1], x_recv.at[q, d - 1], r, 4 * at_x(d) + z)

    def product(q, zt):
        zl, start, rows = CHUNKS[q]
        total = None
        for k in range(4):
            part = lax.dot_general(
                zc[zl, k, :, start:start + rows].reshape(4 * rows, 512), sbuf[k, zt].reshape(512, 512),
                (((1,), (1,)), ((), ())), preferred_element_type=F32,
            )
            total = part if total is None else total + part
        return total

    def row_places(q):
        zl, start, rows = CHUNKS[q]
        return [(pl.ds(zl * 384 + p * 96 + start, rows), slice(p * rows, (p + 1) * rows)) for p in range(4)]

    def coupling_part(q):
        zl, start, rows = CHUNKS[q]
        here = pl.ds(start, rows)
        for d in range(1, 4):
            arrived(zc.at[zl, :, at_x(4 - d), here], x_recv.at[q, d - 1])
        for d in FAR_ORDER:
            pbuf[zl, d - 1, :, start:start + rows] = product(q, at_z(d)).astype(BF16).reshape(4, rows, 512)
            send(
                pbuf.at[zl, d - 1, :, here], rz.at[zl, d - 1, :, here],
                z_send.at[q, d - 1], z_recv.at[q, d - 1], r, 4 * x + at_z(d),
            )
        total = product(q, z)
        for place, part in row_places(q):
            out_ref[place, :] = total[part]

    def coupling_done(q):
        zl, start, rows = CHUNKS[q]
        for d in range(3):
            arrived(rz.at[zl, d, :, pl.ds(start, rows)], z_recv.at[q, d])
        for p, (place, part) in enumerate(row_places(q)):
            total = out_ref[place, :]
            for d in range(3):
                total += rz[zl, d, p, start:start + rows].astype(F32)
            total = -total
            out_ref[place, :] = total
            terms = total * zc[zl, x, p, start:start + rows].astype(F32)
            cross[place, :] = terms[:, 0:128] + terms[:, 128:256] + terms[:, 256:384] + terms[:, 384:512]

    for step in range(NQ + 3):
        if step < NQ:
            zeta_part(step)
            zeta_send(step)
        if step == 0:
            s_far(0)
            s_far(1)
        if 0 <= step - 1 < NQ:
            zeta_done(step - 1)
        if step == 2:
            s_all()
        if 0 <= step - 2 < NQ:
            coupling_part(step - 2)
        if 0 <= step - 3 < NQ:
            coupling_done(step - 3)
        if step == NQ:
            for d in range(1, 8):
                arrived(fa.at[lax.rem(r + 8 - d, 8)], fr_recv.at[d])
            ca[c, 8:16] = jnp.sum(fa[...], axis=0)
            ca[c, 0:8] = jnp.zeros((8, 128), F32)

    sums = jnp.sum(cross[...].T, axis=0, keepdims=True)
    for n in range(6):
        ca[c, n:n + 1] = sums[:, n * 128:(n + 1) * 128]
    for d in range(1, 16):
        send(ca.at[c], ca.at[c], cc_send.at[d], cc_recv.at[d], r, lax.rem(c + d, 16))
    for n in range(6):
        for m in range(4):
            rows, columns = slice(n * 128, (n + 1) * 128), slice(m * 128, (m + 1) * 128)
            out_ref[rows, columns] = out_ref[rows, columns] * block_mask[n][m]
    for d in range(1, 16):
        arrived(ca.at[lax.rem(c + 16 - d, 16)], cc_recv.at[d])
    cb[r] = jnp.sum(ca[:, 0:8], axis=0)
    for d in range(1, 8):
        send(cb.at[r], cb.at[r], cr_send.at[d], cr_recv.at[d], lax.rem(r + d, 8), c)
    wanted = jnp.broadcast_to(owner_ref[...].astype(F32), (128, 48)).T
    lanes = lax.broadcasted_iota(jnp.int32, (48, 128), 1).astype(F32)
    for d in range(1, 8):
        arrived(cb.at[lax.rem(r + 8 - d, 8)], cr_recv.at[d])
    picked = jnp.zeros((48, 128), F32)
    for n in range(48):
        row = jnp.log(ca[n // 3, 8 + n % 3:9 + n % 3] - cb[n // 6, n % 6:n % 6 + 1])
        picked = jnp.where(wanted - float(128 * n) == lanes, row, picked)
    log_ref[...] = jnp.sum(picked.T, axis=0, keepdims=True)

    @pl.when(same)
    def _():
        for copy in factor_copies(0) + sigma_copy(1 - lax.rem(z, 2)) + spread_copies():
            copy.wait_send()

    @pl.when(other)
    def _():
        for copy in factor_copies(1) + sigma_copy(0) + sigma_copy(1):
            copy.wait_send()

    for copy in pending:
        copy.wait_send()


def per_device(sigma_ss, l_cs, g_cc, pattern, sup_sizes, owner):
    dma = pltpu.SemaphoreType.DMA
    any_space = pl.BlockSpec(memory_space=pl.ANY)
    vmem = pl.BlockSpec(memory_space=pltpu.VMEM)
    smem = pl.BlockSpec(memory_space=pltpu.SMEM)
    sel_cs, log_var = pl.pallas_call(
        kernel,
        out_shape=(
            jax.ShapeDtypeStruct((768, 512), F32),
            jax.ShapeDtypeStruct((1, 48), F32),
        ),
        in_specs=[any_space, vmem, vmem, vmem, smem, vmem],
        out_specs=(vmem, vmem),
        scratch_shapes=[
            pltpu.VMEM((4, 96, 768), BF16),
            pltpu.VMEM((2, 4, 2, 96, 768), BF16),
            pltpu.VMEM((2, 4, 2, 384, 512), BF16),
            pltpu.VMEM((4, 4, 2, 256, 512), BF16),
            pltpu.VMEM((2, 4, 4, 96, 512), F32),
            pltpu.VMEM((2, 3, 96, 2176), jnp.int16),
            pltpu.VMEM((2, 3, 96, 2176), jnp.int16),
            pltpu.VMEM((2, 4, 4, 96, 512), BF16),
            pltpu.VMEM((2, 3, 4, 96, 512), BF16),
            pltpu.VMEM((2, 3, 4, 96, 512), BF16),
            pltpu.VMEM((768, 128), F32),
            pltpu.VMEM((8, 128), F32),
            pltpu.VMEM((8, 8, 128), F32),
            pltpu.VMEM((16, 16, 128), F32),
            pltpu.VMEM((8, 8, 128), F32),
            dma((3,)),
            dma((4,)), dma((4, 2)), dma((4,)), dma((2,)),
            dma((6,)), dma((6,)), dma((4,)), dma((4,)),
            dma((2, 2)), dma((2, 2)), dma((2, 6)), dma((2, 6)), dma((2, 4)), dma((2, 4)),
            dma((NQ, 3)), dma((NQ, 3)), dma((NQ, 3)), dma((NQ, 3)), dma((NQ, 3)), dma((NQ, 3)),
            dma((8,)), dma((8,)),
            dma((8,)), dma((8,)), dma((16,)), dma((16,)),
        ],
        compiler_params=pltpu.CompilerParams(
            collective_id=0, has_side_effects=True, vmem_limit_bytes=60 * 1024 * 1024
        ),
    )(sigma_ss, l_cs, g_cc, pattern, sup_sizes, owner.reshape(1, 48))
    return (sel_cs, log_var.reshape(48))


def solution(mesh):
    in_specs = (
        P("col", "row"),
        P("row", "col"),
        P("row", "col"),
        P(None, "col"),
        P(),
        P(("row", "col")),
    )
    out_specs = (P("row", "col"), P(("row", "col")))
    return jax.shard_map(
        per_device, mesh=mesh, in_specs=in_specs, out_specs=out_specs, check_vma=False
    )
```

```python
import jax
import jax.numpy as jnp
from jax import lax
from jax.experimental import pallas as pl
from jax.experimental.pallas import tpu as pltpu
from jax.sharding import PartitionSpec as P

NSUP = 16
MESH = pl.DeviceIdType.MESH
F32 = jnp.float32
BF16 = jnp.bfloat16
PASSES = ((0, 0, 32), (0, 32, 64), (1, 0, 96))
PASS_PIECES = ((0, 1), (2, 3), (4, 5, 6, 7))
PIECES = (
    (0, 0, 16), (0, 16, 16), (0, 32, 32), (0, 64, 32),
    (1, 0, 32), (1, 32, 32), (1, 64, 16), (1, 80, 16),
)
CHUNKS = ((0, 0, 32), (0, 32, 32), (0, 64, 32), (1, 0, 32), (1, 32, 32), (1, 64, 16), (1, 80, 16))
CHUNK_PIECES = ((0, 1), (2,), (3,), (4,), (5,), (6,), (7,))
ORDER = (
    "d0 d1 d2 c0 d3 c1 f0 d4 c2 d5 f1 d6 c3 d7 f2 c4 c5 f3 c6 f4 f5 f6"
).split()
NP = len(PIECES)
NQ = len(CHUNKS)
FAR_ORDER = (2, 1, 3)


def kernel(
    sigma_ref, l_ref, g_ref, pattern_ref, sizes_ref, owner_ref,
    out_ref, log_ref,
    gt_ref, gbuf, mbuf, sbuf, acc, ysend, yrecv, zc, pbuf, rz, cross, fac_ref, fa, ca, cb,
    local_sem, ga_send, ga_recv, gg_send, gg_recv,
    m_send, m_recv, m_sib_send, m_sib_recv,
    sa_send, sa_recv, s_send, s_recv, s_sib_send, s_sib_recv,
    y_send, y_recv, x_send, x_recv, z_send, z_recv,
    fr_send, fr_recv, cr_send, cr_recv, cc_send, cc_recv,
):
    r = lax.axis_index("row")
    c = lax.axis_index("col")
    y, i = r // 2, r % 2
    x, z = c // 4, c % 4
    sib = 2 * y + 1 - i
    t = z // 2
    same = i == t
    other = i != t

    def at_x(d):
        return lax.rem(x + d, 4)

    def at_y(d):
        return lax.rem(y + d, 4)

    def at_z(d):
        return lax.rem(z + d, 4)

    def remote(src, dst, send, recv, row, col):
        return pltpu.make_async_remote_copy(
            src_ref=src, dst_ref=dst, send_sem=send, recv_sem=recv,
            device_id=(row, col), device_id_type=MESH,
        )

    def arrived(dst, recv):
        pltpu.make_async_copy(dst, dst, recv).wait()

    pending = []

    def send(*args):
        copy = remote(*args)
        copy.start()
        pending.append(copy)

    barrier = pltpu.get_barrier_semaphore()
    partners = [(r, lax.rem(c + d, 16)) for d in range(1, 16)]
    partners += [(lax.rem(r + d, 8), c) for d in range(1, 8)]
    partners += [(sib, 4 * at_x(d) + z) for d in range(1, 4)]
    partners += [(sib, 4 * x + at_z(d)) for d in range(1, 4)]
    for partner in partners:
        pl.semaphore_signal(barrier, inc=1, device_id=partner, device_id_type=MESH)

    ends, total_size = [], jnp.int32(0)
    for s in range(NSUP):
        total_size = total_size + sizes_ref[s]
        ends.append(total_size)
    pattern = pattern_ref[...].astype(F32)
    block_mask = []
    for n in range(6):
        place = jnp.int32(0)
        for s in range(NSUP):
            place = place + (ends[s] <= 6 * r + n).astype(jnp.int32)
        place = jnp.minimum(place, NSUP - 1)
        lane = lax.broadcasted_iota(jnp.int32, (4, NSUP), 1)
        column = jnp.sum(jnp.where(lane == place, pattern, 0.0), axis=1, keepdims=True)
        block_mask.append([column[m:m + 1] for m in range(4)])

    for n in range(6):
        for m in range(4):
            block = l_ref[n * 128:(n + 1) * 128, m * 128:(m + 1) * 128].astype(F32)
            mbuf[i, x, n // 3, (n % 3) * 128:(n % 3 + 1) * 128, m * 128:(m + 1) * 128] = (
                block * block_mask[n][m]
            ).astype(BF16)
    gt_ref[...] = g_ref[...].T.reshape(4, 96, 768)
    wide = g_ref[...].astype(F32)
    squares = jnp.sum(wide * wide, axis=0, keepdims=True)
    fac_ref[...] = jnp.zeros((8, 128), F32)
    for n in range(3):
        fac_ref[n:n + 1] = squares[:, n * 128:(n + 1) * 128]

    pl.semaphore_wait(barrier, len(partners))

    fa[r] = fac_ref[...]
    for d in range(1, 8):
        send(fac_ref, fa.at[r], fr_send.at[d], fr_recv.at[d], lax.rem(r + d, 8), c)

    def factor_dst():
        return gbuf.at[lax.rem(z, 2), x, i]

    def factor_copies(rel):
        copies = []
        for d in range(0 if rel else 1, 4):
            copies.append(remote(
                gt_ref.at[at_x(d)], factor_dst(), ga_send.at[d], ga_recv.at[d, rel],
                2 * y + t, 4 * at_x(d) + z,
            ))
        return copies

    @pl.when(same)
    def _():
        pltpu.make_async_copy(gt_ref.at[x], factor_dst(), local_sem.at[0]).start()
        for copy in factor_copies(0):
            copy.start()

    @pl.when(other)
    def _():
        for copy in factor_copies(1):
            copy.start()

    def sigma_part(l, half):
        return sigma_ref.at[pl.ds(half * 256, 256), pl.ds(pl.multiple_of(l * 512, 512), 512)]

    def sigma_own():
        return [
            pltpu.make_async_copy(sigma_part(lax.rem(z, 2), h), sbuf.at[y, z, h], local_sem.at[1 + h])
            for h in range(2)
        ]

    def sigma_copy(l):
        return [
            remote(
                sigma_part(l, h), sbuf.at[y, z, h],
                sa_send.at[l, h], sa_recv.at[lax.rem(z, 2), h], 2 * y + t, 4 * x + 2 * i + l,
            )
            for h in range(2)
        ]

    @pl.when(same)
    def _():
        for copy in sigma_own() + sigma_copy(1 - lax.rem(z, 2)):
            copy.start()

    @pl.when(other)
    def _():
        for first, second in zip(sigma_copy(0), sigma_copy(1)):
            first.start()
            second.start()

    def ring_first(src, slot, snd, rcv, right, left, me):
        send(src(0), slot(me, 0), snd.at[0], rcv.at[0], *right)
        send(src(1), slot(me, 1), snd.at[2], rcv.at[2], *left)
        send(src(1), slot(me, 1), snd.at[1], rcv.at[1], *right)
        send(src(0), slot(me, 0), snd.at[3], rcv.at[3], *left)

    def ring_forward(slot, snd, rcv, right, left, at):
        arrived(slot(at(3), 0), rcv.at[0])
        send(slot(at(3), 0), slot(at(3), 0), snd.at[4], rcv.at[4], *right)
        arrived(slot(at(1), 1), rcv.at[2])
        send(slot(at(1), 1), slot(at(1), 1), snd.at[5], rcv.at[5], *left)

    def ring_rest(slot, rcv, at):
        arrived(slot(at(3), 1), rcv.at[1])
        arrived(slot(at(1), 0), rcv.at[3])

    def ring_far(slot, rcv, at):
        arrived(slot(at(2), 0), rcv.at[4])
        arrived(slot(at(2), 1), rcv.at[5])

    x_right, x_left = (r, 4 * at_x(1) + z), (r, 4 * at_x(3) + z)
    y_right, y_left = (2 * at_y(1) + i, c), (2 * at_y(3) + i, c)

    def m_slot(place, half):
        return mbuf.at[i, place, half]

    def m_share(n, place):
        send(mbuf.at[i, place], mbuf.at[i, place], m_sib_send.at[n], m_sib_recv.at[n], sib, c)

    s_block = [jnp.where(same, lax.rem(z, 2), 0)]
    s_block.append(1 - s_block[0])

    def s_slot(order):
        return lambda place, half: sbuf.at[place, 2 * i + s_block[order], half]

    def s_share(order, n, place):
        block = sbuf.at[place, 2 * i + s_block[order]]
        send(block, block, s_sib_send.at[order, n], s_sib_recv.at[order, n], sib, c)

    def s_first(order):
        slot = s_slot(order)
        snd, rcv = s_send.at[order], s_recv.at[order]
        ring_first(lambda h: slot(y, h), slot, snd, rcv, y_right, y_left, y)
        s_share(order, 0, y)

    def s_forward(order):
        ring_forward(s_slot(order), s_send.at[order], s_recv.at[order], y_right, y_left, at_y)

    def s_rest(order):
        ring_rest(s_slot(order), s_recv.at[order], at_y)
        s_share(order, 1, at_y(3))
        s_share(order, 2, at_y(1))

    def s_far(order):
        ring_far(s_slot(order), s_recv.at[order], at_y)
        s_share(order, 3, at_y(2))

    def s_all():
        for order in range(2):
            for n, d in enumerate((0, 3, 1, 2)):
                place = 2 * (1 - i) + sib_block[order]
                arrived(sbuf.at[at_y(d), place], s_sib_recv.at[order, n])

    sib_block = [jnp.where(other, lax.rem(z, 2), 0)]
    sib_block.append(1 - sib_block[0])

    ring_first(lambda h: m_slot(x, h), m_slot, m_send, m_recv, x_right, x_left, x)
    m_share(0, x)

    @pl.when(same)
    def _():
        for copy in sigma_own():
            copy.wait()

    @pl.when(other)
    def _():
        for h in range(2):
            arrived(sbuf.at[y, 2 * i, h], sa_recv.at[0, h])

    s_first(0)

    for h in range(2):
        arrived(sbuf.at[y, 2 * i + s_block[1], h], sa_recv.at[s_block[1], h])
    s_first(1)

    def g_half(zl, half):
        return gbuf.at[zl, pl.ds(2 * half, 2)]

    def g_copy(zl, half, n, d):
        return remote(
            g_half(zl, half), g_half(zl, half), gg_send.at[zl, n], gg_recv.at[zl, n],
            r, 4 * x + at_z(d),
        )

    def g_source(zl):
        return [g_copy(zl, 0, 0, 1), g_copy(zl, 1, 2, 3), g_copy(zl, 1, 1, 1), g_copy(zl, 0, 3, 3)]

    def g_from(zl):
        return lax.rem(z + 4 - (2 * i + zl), 4)

    @pl.when(same)
    def _():
        pltpu.make_async_copy(gt_ref.at[x], factor_dst(), local_sem.at[0]).wait()
        for d in range(4):
            for rel in range(2):
                if d or rel:
                    src_core = 1 - i if rel else i
                    arrived(gbuf.at[lax.rem(z, 2), at_x(4 - d), src_core], ga_recv.at[d, rel])

    for zl in range(2):
        @pl.when(g_from(zl) == 0)
        def _():
            for copy in g_source(zl):
                copy.start()

    def g_forward():
        for zl in range(2):
            @pl.when(g_from(zl) == 1)
            def _():
                arrived(g_half(zl, 0), gg_recv.at[zl, 0])
                g_copy(zl, 0, 4, 1).start()

            @pl.when(g_from(zl) == 3)
            def _():
                arrived(g_half(zl, 1), gg_recv.at[zl, 2])
                g_copy(zl, 1, 5, 3).start()

    def g_rest():
        for zl in range(2):
            @pl.when(g_from(zl) == 1)
            def _():
                arrived(g_half(zl, 1), gg_recv.at[zl, 1])

            @pl.when(g_from(zl) == 3)
            def _():
                arrived(g_half(zl, 0), gg_recv.at[zl, 3])

            @pl.when(g_from(zl) == 2)
            def _():
                arrived(g_half(zl, 0), gg_recv.at[zl, 4])
                arrived(g_half(zl, 1), gg_recv.at[zl, 5])

    def g_sent():
        for zl in range(2):
            @pl.when(g_from(zl) == 0)
            def _():
                for copy in g_source(zl):
                    copy.wait_send()

            @pl.when(g_from(zl) == 1)
            def _():
                g_copy(zl, 0, 4, 1).wait_send()

            @pl.when(g_from(zl) == 3)
            def _():
                g_copy(zl, 1, 5, 3).wait_send()

    s_forward(0)
    g_forward()
    ring_forward(m_slot, m_send, m_recv, x_right, x_left, at_x)
    ring_rest(m_slot, m_recv, at_x)
    m_share(1, at_x(3))
    m_share(2, at_x(1))
    s_rest(0)
    s_forward(1)
    s_rest(1)

    ring_far(m_slot, m_recv, at_x)
    m_share(3, at_x(2))
    g_rest()
    for n, d in enumerate((0, 3, 1, 2)):
        arrived(mbuf.at[1 - i, at_x(d)], m_sib_recv.at[n])

    def zeta_part(q):
        zl, start, rows = PASSES[q]
        here = slice(start, start + rows)
        g0 = gbuf[zl, :, 0, here].reshape(4 * rows, 768)
        g1 = gbuf[zl, :, 1, here].reshape(4 * rows, 768)

        def step(k, carry):
            total = jnp.dot(g0, mbuf[0, k].reshape(768, 512), preferred_element_type=F32)
            total += jnp.dot(g1, mbuf[1, k].reshape(768, 512), preferred_element_type=F32)
            acc[zl, :, k, here] = total.reshape(4, rows, 512)
            return carry

        lax.fori_loop(0, 4, step, 0)

    def zeta_send(q):
        zl, start, rows = PIECES[q]
        here = slice(start, start + rows)
        for d in FAR_ORDER:
            parts = [acc[zl, at_y(d), k, here] for k in range(4)]
            top = jnp.abs(parts[0])
            for part in parts[1:]:
                top = jnp.maximum(top, jnp.abs(part))
            top = jnp.max(top, axis=1, keepdims=True)
            power = jnp.floor(jnp.log2(jnp.maximum(top, 1e-30)) + 1.01)
            up = jnp.exp2(15.0 - power)
            for k in range(4):
                code = jnp.round(parts[k] * up).astype(jnp.int32).astype(jnp.int16)
                ysend[zl, d - 1, here, k * 512:(k + 1) * 512] = code
            ysend[zl, d - 1, here, 2048:] = jnp.broadcast_to(
                power.astype(jnp.int32), (rows, 128)
            ).astype(jnp.int16)
            send(
                ysend.at[zl, d - 1, pl.ds(start, rows)], yrecv.at[zl, d - 1, pl.ds(start, rows)],
                y_send.at[q, d - 1], y_recv.at[q, d - 1], 2 * at_y(d) + i, c,
            )

    def zeta_done(q):
        zl, start, rows = PIECES[q]
        here = slice(start, start + rows)
        for d in range(3):
            arrived(yrecv.at[zl, d, pl.ds(start, rows)], y_recv.at[q, d])
        down = []
        for d in range(3):
            power = yrecv[zl, d, here, 2048:].astype(jnp.int32).astype(F32)
            down.append(jnp.exp2(power - 15.0)[:, 0:1])
        for k in range(4):
            total = acc[zl, y, k, here]
            for d in range(3):
                code = yrecv[zl, d, here, k * 512:(k + 1) * 512]
                total += code.astype(jnp.int32).astype(F32) * down[d]
            zc[zl, k, x, here] = total.astype(BF16)
        block = zc.at[zl, :, x, pl.ds(start, rows)]
        for d in FAR_ORDER:
            send(block, block, x_send.at[q, d - 1], x_recv.at[q, d - 1], r, 4 * at_x(d) + z)

    def product(q, zt):
        zl, start, rows = CHUNKS[q]
        total = None
        for k in range(4):
            part = lax.dot_general(
                zc[zl, k, :, start:start + rows].reshape(4 * rows, 512), sbuf[k, zt].reshape(512, 512),
                (((1,), (1,)), ((), ())), preferred_element_type=F32,
            )
            total = part if total is None else total + part
        return total

    def row_places(q):
        zl, start, rows = CHUNKS[q]
        return [(pl.ds(zl * 384 + p * 96 + start, rows), slice(p * rows, (p + 1) * rows)) for p in range(4)]

    def coupling_part(q):
        zl, start, rows = CHUNKS[q]
        here = pl.ds(start, rows)
        for piece in CHUNK_PIECES[q]:
            _, first, some = PIECES[piece]
            for d in range(1, 4):
                arrived(zc.at[zl, :, at_x(4 - d), pl.ds(first, some)], x_recv.at[piece, d - 1])
        for d in FAR_ORDER:
            pbuf[zl, d - 1, :, start:start + rows] = product(q, at_z(d)).astype(BF16).reshape(4, rows, 512)
            send(
                pbuf.at[zl, d - 1, :, here], rz.at[zl, d - 1, :, here],
                z_send.at[q, d - 1], z_recv.at[q, d - 1], r, 4 * x + at_z(d),
            )
        total = product(q, z)
        for place, part in row_places(q):
            out_ref[place, :] = total[part]

    def coupling_done(q):
        zl, start, rows = CHUNKS[q]
        for d in range(3):
            arrived(rz.at[zl, d, :, pl.ds(start, rows)], z_recv.at[q, d])
        for p, (place, part) in enumerate(row_places(q)):
            total = out_ref[place, :]
            for d in range(3):
                total += rz[zl, d, p, start:start + rows].astype(F32)
            total = -total
            out_ref[place, :] = total
            terms = total * zc[zl, x, p, start:start + rows].astype(F32)
            cross[place, :] = terms[:, 0:128] + terms[:, 128:256] + terms[:, 256:384] + terms[:, 384:512]

    for n, pieces in enumerate(PASS_PIECES):
        zeta_part(n)
        for piece in pieces:
            zeta_send(piece)
        if n == 0:
            s_far(0)
        if n == 1:
            s_far(1)
    for item in ORDER:
        n = int(item[1])
        if item == "c0":
            s_all()
        if item == "f4":
            for d in range(1, 8):
                arrived(fa.at[lax.rem(r + 8 - d, 8)], fr_recv.at[d])
            ca[c, 8:16] = jnp.sum(fa[...], axis=0)
            ca[c, 0:8] = jnp.zeros((8, 128), F32)
        {"d": zeta_done, "c": coupling_part, "f": coupling_done}[item[0]](n)

    sums = jnp.sum(cross[...].T, axis=0, keepdims=True)
    for n in range(6):
        ca[c, n:n + 1] = sums[:, n * 128:(n + 1) * 128]
    for d in range(1, 16):
        send(ca.at[c], ca.at[c], cc_send.at[d], cc_recv.at[d], r, lax.rem(c + d, 16))
    for n in range(6):
        for m in range(4):
            rows, columns = slice(n * 128, (n + 1) * 128), slice(m * 128, (m + 1) * 128)
            out_ref[rows, columns] = out_ref[rows, columns] * block_mask[n][m]
    for d in range(1, 16):
        arrived(ca.at[lax.rem(c + 16 - d, 16)], cc_recv.at[d])
    cb[r] = jnp.sum(ca[:, 0:8], axis=0)
    for d in range(1, 8):
        send(cb.at[r], cb.at[r], cr_send.at[d], cr_recv.at[d], lax.rem(r + d, 8), c)
    wanted = jnp.broadcast_to(owner_ref[...].astype(F32), (128, 48)).T
    lanes = lax.broadcasted_iota(jnp.int32, (48, 128), 1).astype(F32)
    for d in range(1, 8):
        arrived(cb.at[lax.rem(r + 8 - d, 8)], cr_recv.at[d])
    picked = jnp.zeros((48, 128), F32)
    for n in range(48):
        row = jnp.log(ca[n // 3, 8 + n % 3:9 + n % 3] - cb[n // 6, n % 6:n % 6 + 1])
        picked = jnp.where(wanted - float(128 * n) == lanes, row, picked)
    log_ref[...] = jnp.sum(picked.T, axis=0, keepdims=True)

    @pl.when(same)
    def _():
        for copy in factor_copies(0) + sigma_copy(1 - lax.rem(z, 2)):
            copy.wait_send()

    @pl.when(other)
    def _():
        for copy in factor_copies(1) + sigma_copy(0) + sigma_copy(1):
            copy.wait_send()

    g_sent()
    for copy in pending:
        copy.wait_send()


def per_device(sigma_ss, l_cs, g_cc, pattern, sup_sizes, owner):
    dma = pltpu.SemaphoreType.DMA
    any_space = pl.BlockSpec(memory_space=pl.ANY)
    vmem = pl.BlockSpec(memory_space=pltpu.VMEM)
    smem = pl.BlockSpec(memory_space=pltpu.SMEM)
    sel_cs, log_var = pl.pallas_call(
        kernel,
        out_shape=(
            jax.ShapeDtypeStruct((768, 512), F32),
            jax.ShapeDtypeStruct((1, 48), F32),
        ),
        in_specs=[any_space, vmem, vmem, vmem, smem, vmem],
        out_specs=(vmem, vmem),
        scratch_shapes=[
            pltpu.VMEM((4, 96, 768), BF16),
            pltpu.VMEM((2, 4, 2, 96, 768), BF16),
            pltpu.VMEM((2, 4, 2, 384, 512), BF16),
            pltpu.VMEM((4, 4, 2, 256, 512), BF16),
            pltpu.VMEM((2, 4, 4, 96, 512), F32),
            pltpu.VMEM((2, 3, 96, 2176), jnp.int16),
            pltpu.VMEM((2, 3, 96, 2176), jnp.int16),
            pltpu.VMEM((2, 4, 4, 96, 512), BF16),
            pltpu.VMEM((2, 3, 4, 96, 512), BF16),
            pltpu.VMEM((2, 3, 4, 96, 512), BF16),
            pltpu.VMEM((768, 128), F32),
            pltpu.VMEM((8, 128), F32),
            pltpu.VMEM((8, 8, 128), F32),
            pltpu.VMEM((16, 16, 128), F32),
            pltpu.VMEM((8, 8, 128), F32),
            dma((3,)),
            dma((4,)), dma((4, 2)), dma((2, 6)), dma((2, 6)),
            dma((6,)), dma((6,)), dma((4,)), dma((4,)),
            dma((2, 2)), dma((2, 2)), dma((2, 6)), dma((2, 6)), dma((2, 4)), dma((2, 4)),
            dma((NP, 3)), dma((NP, 3)), dma((NP, 3)), dma((NP, 3)), dma((NQ, 3)), dma((NQ, 3)),
            dma((8,)), dma((8,)),
            dma((8,)), dma((8,)), dma((16,)), dma((16,)),
        ],
        compiler_params=pltpu.CompilerParams(
            collective_id=0, has_side_effects=True, vmem_limit_bytes=60 * 1024 * 1024
        ),
    )(sigma_ss, l_cs, g_cc, pattern.T, sup_sizes, owner.reshape(1, 48))
    return (sel_cs, log_var.reshape(48))


def solution(mesh):
    in_specs = (
        P("col", "row"),
        P("row", "col"),
        P("row", "col"),
        P(None, "col"),
        P(),
        P(("row", "col")),
    )
    out_specs = (P("row", "col"), P(("row", "col")))
    return jax.shard_map(
        per_device, mesh=mesh, in_specs=in_specs, out_specs=out_specs, check_vma=False
    )
```

```python
import jax
import jax.numpy as jnp
from jax import lax
from jax.experimental import pallas as pl
from jax.experimental.pallas import tpu as pltpu
from jax.sharding import PartitionSpec as P

NSUP = 16
MESH = pl.DeviceIdType.MESH
F32 = jnp.float32
BF16 = jnp.bfloat16
PASSES = ((0, 0, 32), (0, 32, 64), (1, 0, 96))
PASS_PIECES = ((0,), (1, 2), (3, 4, 5, 6))
PIECES = (
    (0, 0, 32), (0, 32, 32), (0, 64, 32),
    (1, 0, 32), (1, 32, 32), (1, 64, 16), (1, 80, 16),
)
CHUNKS = ((0, 0, 32), (0, 32, 32), (0, 64, 32), (1, 0, 32), (1, 32, 32), (1, 64, 16), (1, 80, 16))
CHUNK_PIECES = ((0,), (1,), (2,), (3,), (4,), (5,), (6,))
ORDER = (
    ("d", 0), ("d", 1), ("c", 0), ("d", 2), ("c", 1), ("f", 0), ("d", 3), ("c", 2), ("d", 4),
    ("f", 1), ("d", 5), ("c", 3), ("d", 6), ("f", 2), ("c", 4), ("c", 5), ("f", 3), ("c", 6), ("f", 4),
    ("f", 5), ("f", 6),
)
NP = len(PIECES)
NQ = len(CHUNKS)
FAR_ORDER = (2, 1, 3)


def kernel(
    sigma_ref, l_hbm, g_hbm, pattern_ref, sizes_ref, owner_ref,
    sel_ref, log_ref,
    out_ref, l_ref, g_ref, gt_ref, gbuf, mbuf, sbuf, acc, ysend, yrecv, zc, pbuf, rz, cross, fac_ref, fa, ca, cb,
    local_sem, out_sem, ga_send, ga_recv, gg_send, gg_recv,
    m_send, m_recv, m_sib_send, m_sib_recv,
    sa_send, sa_recv, s_send, s_recv, s_sib_send, s_sib_recv,
    y_send, y_recv, x_send, x_recv, z_send, z_recv,
    fr_send, fr_recv, cr_send, cr_recv, cc_send, cc_recv,
):
    r = lax.axis_index("row")
    c = lax.axis_index("col")
    y, i = r // 2, r % 2
    x, z = c // 4, c % 4
    sib = 2 * y + 1 - i
    t = z // 2
    same = i == t
    other = i != t

    def at_x(d):
        return lax.rem(x + d, 4)

    def at_y(d):
        return lax.rem(y + d, 4)

    def at_z(d):
        return lax.rem(z + d, 4)

    def remote(src, dst, send, recv, row, col):
        return pltpu.make_async_remote_copy(
            src_ref=src, dst_ref=dst, send_sem=send, recv_sem=recv,
            device_id=(row, col), device_id_type=MESH,
        )

    def arrived(dst, recv):
        pltpu.make_async_copy(dst, dst, recv).wait()

    pending = []

    def send(*args):
        copy = remote(*args)
        copy.start()
        pending.append(copy)

    def sent():
        for copy in pending:
            copy.wait_send()
        pending.clear()

    barrier = pltpu.get_barrier_semaphore()
    partners = [(r, lax.rem(c + d, 16)) for d in range(1, 16)]
    partners += [(lax.rem(r + d, 8), c) for d in range(1, 8)]
    partners += [(sib, 4 * at_x(d) + z) for d in range(1, 4)]
    partners += [(sib, 4 * x + at_z(d)) for d in range(1, 4)]
    for partner in partners:
        pl.semaphore_signal(barrier, inc=1, device_id=partner, device_id_type=MESH)
    l_copy = pltpu.make_async_copy(l_hbm, l_ref, local_sem.at[3])
    g_copy_in = pltpu.make_async_copy(g_hbm, g_ref, local_sem.at[4])
    g_copy_in.start()
    l_copy.start()

    ends, total_size = [], jnp.int32(0)
    for s in range(NSUP):
        total_size = total_size + sizes_ref[s]
        ends.append(total_size)
    pattern = pattern_ref[...].astype(F32)
    block_mask = []
    for n in range(6):
        place = jnp.int32(0)
        for s in range(NSUP):
            place = place + (ends[s] <= 6 * r + n).astype(jnp.int32)
        place = jnp.minimum(place, NSUP - 1)
        lane = lax.broadcasted_iota(jnp.int32, (4, NSUP), 1)
        column = jnp.sum(jnp.where(lane == place, pattern, 0.0), axis=1, keepdims=True)
        block_mask.append([column[m:m + 1] for m in range(4)])

    g_copy_in.wait()
    gt_ref[...] = g_ref[...].T.reshape(4, 96, 768)
    wide = g_ref[...].astype(F32)
    squares = jnp.sum(wide * wide, axis=0, keepdims=True)
    fac_ref[...] = jnp.zeros((8, 128), F32)
    for n in range(3):
        fac_ref[n:n + 1] = squares[:, n * 128:(n + 1) * 128]

    l_copy.wait()
    for n in range(6):
        for m in range(4):
            block = l_ref[n * 128:(n + 1) * 128, m * 128:(m + 1) * 128].astype(F32)
            mbuf[i, x, n // 3, (n % 3) * 128:(n % 3 + 1) * 128, m * 128:(m + 1) * 128] = (
                block * block_mask[n][m]
            ).astype(BF16)
    pl.semaphore_wait(barrier, len(partners))

    fa[r] = fac_ref[...]
    for d in range(1, 8):
        send(fac_ref, fa.at[r], fr_send.at[d], fr_recv.at[d], lax.rem(r + d, 8), c)

    def factor_dst():
        return gbuf.at[lax.rem(z, 2), x, i]

    def factor_copies(rel):
        copies = []
        for d in range(0 if rel else 1, 4):
            copies.append(remote(
                gt_ref.at[at_x(d)], factor_dst(), ga_send.at[d], ga_recv.at[d, rel],
                2 * y + t, 4 * at_x(d) + z,
            ))
        return copies

    @pl.when(same)
    def _():
        pltpu.make_async_copy(gt_ref.at[x], factor_dst(), local_sem.at[0]).start()
        for copy in factor_copies(0):
            copy.start()

    @pl.when(other)
    def _():
        for copy in factor_copies(1):
            copy.start()

    def sigma_part(l, half):
        return sigma_ref.at[pl.ds(half * 256, 256), pl.ds(pl.multiple_of(l * 512, 512), 512)]

    def sigma_own():
        return [
            pltpu.make_async_copy(sigma_part(lax.rem(z, 2), h), sbuf.at[y, z, h], local_sem.at[1 + h])
            for h in range(2)
        ]

    def sigma_copy(l):
        return [
            remote(
                sigma_part(l, h), sbuf.at[y, z, h],
                sa_send.at[l, h], sa_recv.at[lax.rem(z, 2), h], 2 * y + t, 4 * x + 2 * i + l,
            )
            for h in range(2)
        ]

    @pl.when(same)
    def _():
        for copy in sigma_own() + sigma_copy(1 - lax.rem(z, 2)):
            copy.start()

    @pl.when(other)
    def _():
        for first, second in zip(sigma_copy(0), sigma_copy(1)):
            first.start()
            second.start()

    def ring_first(src, slot, snd, rcv, right, left, me):
        send(src(0), slot(me, 0), snd.at[0], rcv.at[0], *right)
        send(src(1), slot(me, 1), snd.at[2], rcv.at[2], *left)
        send(src(1), slot(me, 1), snd.at[1], rcv.at[1], *right)
        send(src(0), slot(me, 0), snd.at[3], rcv.at[3], *left)

    def ring_forward(slot, snd, rcv, right, left, at):
        arrived(slot(at(3), 0), rcv.at[0])
        send(slot(at(3), 0), slot(at(3), 0), snd.at[4], rcv.at[4], *right)
        arrived(slot(at(1), 1), rcv.at[2])
        send(slot(at(1), 1), slot(at(1), 1), snd.at[5], rcv.at[5], *left)

    def ring_rest(slot, rcv, at):
        arrived(slot(at(3), 1), rcv.at[1])
        arrived(slot(at(1), 0), rcv.at[3])

    def ring_far(slot, rcv, at):
        arrived(slot(at(2), 0), rcv.at[4])
        arrived(slot(at(2), 1), rcv.at[5])

    x_right, x_left = (r, 4 * at_x(1) + z), (r, 4 * at_x(3) + z)
    y_right, y_left = (2 * at_y(1) + i, c), (2 * at_y(3) + i, c)

    def m_slot(place, half):
        return mbuf.at[i, place, half]

    def m_share(n, place):
        send(mbuf.at[i, place], mbuf.at[i, place], m_sib_send.at[n], m_sib_recv.at[n], sib, c)

    s_block = [jnp.where(same, lax.rem(z, 2), 0)]
    s_block.append(1 - s_block[0])

    def s_slot(order):
        return lambda place, half: sbuf.at[place, 2 * i + s_block[order], half]

    def s_share(order, n, place):
        block = sbuf.at[place, 2 * i + s_block[order]]
        send(block, block, s_sib_send.at[order, n], s_sib_recv.at[order, n], sib, c)

    def s_first(order):
        slot = s_slot(order)
        snd, rcv = s_send.at[order], s_recv.at[order]
        ring_first(lambda h: slot(y, h), slot, snd, rcv, y_right, y_left, y)
        s_share(order, 0, y)

    def s_forward(order):
        ring_forward(s_slot(order), s_send.at[order], s_recv.at[order], y_right, y_left, at_y)

    def s_rest(order):
        ring_rest(s_slot(order), s_recv.at[order], at_y)
        s_share(order, 1, at_y(3))
        s_share(order, 2, at_y(1))

    def s_far(order):
        ring_far(s_slot(order), s_recv.at[order], at_y)
        s_share(order, 3, at_y(2))

    def s_all():
        for order in range(2):
            for n, d in enumerate((0, 3, 1, 2)):
                place = 2 * (1 - i) + sib_block[order]
                arrived(sbuf.at[at_y(d), place], s_sib_recv.at[order, n])

    sib_block = [jnp.where(other, lax.rem(z, 2), 0)]
    sib_block.append(1 - sib_block[0])

    ring_first(lambda h: m_slot(x, h), m_slot, m_send, m_recv, x_right, x_left, x)
    m_share(0, x)

    @pl.when(same)
    def _():
        for copy in sigma_own():
            copy.wait()

    @pl.when(other)
    def _():
        for h in range(2):
            arrived(sbuf.at[y, 2 * i, h], sa_recv.at[0, h])

    s_first(0)

    for h in range(2):
        arrived(sbuf.at[y, 2 * i + s_block[1], h], sa_recv.at[s_block[1], h])
    s_first(1)

    def g_half(zl, half):
        return gbuf.at[zl, pl.ds(2 * half, 2)]

    def g_copy(zl, half, n, d):
        return remote(
            g_half(zl, half), g_half(zl, half), gg_send.at[zl, n], gg_recv.at[zl, n],
            r, 4 * x + at_z(d),
        )

    def g_source(zl):
        return [g_copy(zl, 0, 0, 1), g_copy(zl, 1, 2, 3), g_copy(zl, 1, 1, 1), g_copy(zl, 0, 3, 3)]

    def g_from(zl):
        return lax.rem(z + 4 - (2 * i + zl), 4)

    @pl.when(same)
    def _():
        pltpu.make_async_copy(gt_ref.at[x], factor_dst(), local_sem.at[0]).wait()
        for d in range(4):
            for rel in range(2):
                if d or rel:
                    src_core = 1 - i if rel else i
                    arrived(gbuf.at[lax.rem(z, 2), at_x(4 - d), src_core], ga_recv.at[d, rel])

    for zl in range(2):
        @pl.when(g_from(zl) == 0)
        def _():
            for copy in g_source(zl):
                copy.start()

    def g_forward():
        for zl in range(2):
            @pl.when(g_from(zl) == 1)
            def _():
                arrived(g_half(zl, 0), gg_recv.at[zl, 0])
                g_copy(zl, 0, 4, 1).start()

            @pl.when(g_from(zl) == 3)
            def _():
                arrived(g_half(zl, 1), gg_recv.at[zl, 2])
                g_copy(zl, 1, 5, 3).start()

    def g_rest():
        for zl in range(2):
            @pl.when(g_from(zl) == 1)
            def _():
                arrived(g_half(zl, 1), gg_recv.at[zl, 1])

            @pl.when(g_from(zl) == 3)
            def _():
                arrived(g_half(zl, 0), gg_recv.at[zl, 3])

            @pl.when(g_from(zl) == 2)
            def _():
                arrived(g_half(zl, 0), gg_recv.at[zl, 4])
                arrived(g_half(zl, 1), gg_recv.at[zl, 5])

    def g_sent():
        for zl in range(2):
            @pl.when(g_from(zl) == 0)
            def _():
                for copy in g_source(zl):
                    copy.wait_send()

            @pl.when(g_from(zl) == 1)
            def _():
                g_copy(zl, 0, 4, 1).wait_send()

            @pl.when(g_from(zl) == 3)
            def _():
                g_copy(zl, 1, 5, 3).wait_send()

    s_forward(0)
    g_forward()
    ring_forward(m_slot, m_send, m_recv, x_right, x_left, at_x)
    ring_rest(m_slot, m_recv, at_x)
    m_share(1, at_x(3))
    m_share(2, at_x(1))
    s_rest(0)
    s_forward(1)
    s_rest(1)

    ring_far(m_slot, m_recv, at_x)
    m_share(3, at_x(2))
    g_rest()
    for n, d in enumerate((0, 3, 1, 2)):
        arrived(mbuf.at[1 - i, at_x(d)], m_sib_recv.at[n])

    def zeta_part(q):
        zl, start, rows = PASSES[q]
        here = slice(start, start + rows)
        g0 = gbuf[zl, :, 0, here].reshape(4 * rows, 768)
        g1 = gbuf[zl, :, 1, here].reshape(4 * rows, 768)

        def step(k, carry):
            total = jnp.dot(g0, mbuf[0, k].reshape(768, 512), preferred_element_type=F32)
            total += jnp.dot(g1, mbuf[1, k].reshape(768, 512), preferred_element_type=F32)
            acc[zl, :, k, here] = total.reshape(4, rows, 512)
            return carry

        lax.fori_loop(0, 4, step, 0)

    def zeta_send(q):
        zl, start, rows = PIECES[q]
        here = slice(start, start + rows)
        for d in FAR_ORDER:
            parts = [acc[zl, at_y(d), k, here] for k in range(4)]
            top = jnp.abs(parts[0])
            for part in parts[1:]:
                top = jnp.maximum(top, jnp.abs(part))
            top = jnp.max(top, axis=1, keepdims=True)
            power = jnp.floor(jnp.log2(jnp.maximum(top, 1e-30)) + 1.01)
            up = jnp.exp2(15.0 - power)
            for k in range(4):
                code = jnp.round(parts[k] * up).astype(jnp.int32).astype(jnp.int16)
                ysend[zl, d - 1, here, k * 512:(k + 1) * 512] = code
            ysend[zl, d - 1, here, 2048:] = jnp.broadcast_to(
                power.astype(jnp.int32), (rows, 128)
            ).astype(jnp.int16)
            send(
                ysend.at[zl, d - 1, pl.ds(start, rows)], yrecv.at[zl, d - 1, pl.ds(start, rows)],
                y_send.at[q, d - 1], y_recv.at[q, d - 1], 2 * at_y(d) + i, c,
            )

    def zeta_done(q):
        zl, start, rows = PIECES[q]
        here = slice(start, start + rows)
        for d in range(3):
            arrived(yrecv.at[zl, d, pl.ds(start, rows)], y_recv.at[q, d])
        down = []
        for d in range(3):
            power = yrecv[zl, d, here, 2048:].astype(jnp.int32).astype(F32)
            down.append(jnp.exp2(power - 15.0)[:, 0:1])
        for k in range(4):
            total = acc[zl, y, k, here]
            for d in range(3):
                code = yrecv[zl, d, here, k * 512:(k + 1) * 512]
                total += code.astype(jnp.int32).astype(F32) * down[d]
            zc[zl, k, x, here] = total.astype(BF16)
        block = zc.at[zl, :, x, pl.ds(start, rows)]
        for d in FAR_ORDER:
            send(block, block, x_send.at[q, d - 1], x_recv.at[q, d - 1], r, 4 * at_x(d) + z)

    def product(q, zt):
        zl, start, rows = CHUNKS[q]
        total = None
        for k in range(4):
            part = lax.dot_general(
                zc[zl, k, :, start:start + rows].reshape(4 * rows, 512), sbuf[k, zt].reshape(512, 512),
                (((1,), (1,)), ((), ())), preferred_element_type=F32,
            )
            total = part if total is None else total + part
        return total

    def row_places(q):
        zl, start, rows = CHUNKS[q]
        return [(pl.ds(zl * 384 + p * 96 + start, rows), slice(p * rows, (p + 1) * rows)) for p in range(4)]

    def coupling_part(q):
        zl, start, rows = CHUNKS[q]
        here = pl.ds(start, rows)
        for piece in CHUNK_PIECES[q]:
            _, first, some = PIECES[piece]
            for d in range(1, 4):
                arrived(zc.at[zl, :, at_x(4 - d), pl.ds(first, some)], x_recv.at[piece, d - 1])
        for d in FAR_ORDER:
            pbuf[zl, d - 1, :, start:start + rows] = product(q, at_z(d)).astype(BF16).reshape(4, rows, 512)
            send(
                pbuf.at[zl, d - 1, :, here], rz.at[zl, d - 1, :, here],
                z_send.at[q, d - 1], z_recv.at[q, d - 1], r, 4 * x + at_z(d),
            )
        total = product(q, z)
        for place, part in row_places(q):
            out_ref[place, :] = total[part]

    def out_copy(q, p):
        place = row_places(q)[p][0]
        return pltpu.make_async_copy(out_ref.at[place], sel_ref.at[place], out_sem.at[q, p])

    def coupling_done(q):
        zl, start, rows = CHUNKS[q]
        for d in range(3):
            arrived(rz.at[zl, d, :, pl.ds(start, rows)], z_recv.at[q, d])
        for p, (place, part) in enumerate(row_places(q)):
            total = out_ref[place, :]
            for d in range(3):
                total += rz[zl, d, p, start:start + rows].astype(F32)
            total = -total
            block = (zl * 384 + p * 96 + start) // 128
            out_ref[place, :] = jnp.concatenate(
                [total[:, m * 128:(m + 1) * 128] * block_mask[block][m] for m in range(4)], axis=1
            )
            out_copy(q, p).start()
            terms = total * zc[zl, x, p, start:start + rows].astype(F32)
            cross[place, :] = terms[:, 0:128] + terms[:, 128:256] + terms[:, 256:384] + terms[:, 384:512]

    for n, pieces in enumerate(PASS_PIECES):
        zeta_part(n)
        for piece in pieces:
            zeta_send(piece)
        if n == 0:
            s_far(0)
        if n == 1:
            s_far(1)
    for kind, n in ORDER:
        if (kind, n) == ("c", 0):
            s_all()
        if (kind, n) == ("f", 4):
            for d in range(1, 8):
                arrived(fa.at[lax.rem(r + 8 - d, 8)], fr_recv.at[d])
            ca[c, 8:16] = jnp.sum(fa[...], axis=0)
            ca[c, 0:8] = jnp.zeros((8, 128), F32)
        {"d": zeta_done, "c": coupling_part, "f": coupling_done}[kind](n)

    sums = jnp.sum(cross[...].T, axis=0, keepdims=True)
    for n in range(6):
        ca[c, n:n + 1] = sums[:, n * 128:(n + 1) * 128]
    for d in range(1, 16):
        send(ca.at[c], ca.at[c], cc_send.at[d], cc_recv.at[d], r, lax.rem(c + d, 16))
    @pl.when(same)
    def _():
        for copy in factor_copies(0) + sigma_copy(1 - lax.rem(z, 2)):
            copy.wait_send()

    @pl.when(other)
    def _():
        for copy in factor_copies(1) + sigma_copy(0) + sigma_copy(1):
            copy.wait_send()

    g_sent()
    sent()
    for q in range(NQ):
        for p in range(4):
            out_copy(q, p).wait()
    for d in range(1, 16):
        arrived(ca.at[lax.rem(c + 16 - d, 16)], cc_recv.at[d])
    cb[r] = jnp.sum(ca[:, 0:8], axis=0)
    for d in range(1, 8):
        send(cb.at[r], cb.at[r], cr_send.at[d], cr_recv.at[d], lax.rem(r + d, 8), c)
    wanted = jnp.broadcast_to(owner_ref[...].astype(F32), (128, 48)).T
    lanes = lax.broadcasted_iota(jnp.int32, (48, 128), 1).astype(F32)
    for d in range(1, 8):
        arrived(cb.at[lax.rem(r + 8 - d, 8)], cr_recv.at[d])
    picked = jnp.zeros((48, 128), F32)
    for n in range(48):
        row = jnp.log(ca[n // 3, 8 + n % 3:9 + n % 3] - cb[n // 6, n % 6:n % 6 + 1])
        picked = jnp.where(wanted - float(128 * n) == lanes, row, picked)
    log_ref[...] = jnp.sum(picked.T, axis=0, keepdims=True)

    sent()


def hand_over(from_ref, log_from_ref, to_ref, log_to_ref):
    to_ref[...] = from_ref[...]
    log_to_ref[...] = log_from_ref[...]


def per_device(sigma_ss, l_cs, g_cc, pattern, sup_sizes, owner):
    dma = pltpu.SemaphoreType.DMA
    any_space = pl.BlockSpec(memory_space=pl.ANY)
    vmem = pl.BlockSpec(memory_space=pltpu.VMEM)
    smem = pl.BlockSpec(memory_space=pltpu.SMEM)
    sel_cs, log_var = pl.pallas_call(
        kernel,
        out_shape=(
            jax.ShapeDtypeStruct((768, 512), F32),
            jax.ShapeDtypeStruct((1, 48), F32),
        ),
        in_specs=[any_space, any_space, any_space, vmem, smem, vmem],
        out_specs=(any_space, vmem),
        scratch_shapes=[
            pltpu.VMEM((768, 512), F32),
            pltpu.VMEM((768, 512), BF16),
            pltpu.VMEM((768, 384), BF16),
            pltpu.VMEM((4, 96, 768), BF16),
            pltpu.VMEM((2, 4, 2, 96, 768), BF16),
            pltpu.VMEM((2, 4, 2, 384, 512), BF16),
            pltpu.VMEM((4, 4, 2, 256, 512), BF16),
            pltpu.VMEM((2, 4, 4, 96, 512), F32),
            pltpu.VMEM((2, 3, 96, 2176), jnp.int16),
            pltpu.VMEM((2, 3, 96, 2176), jnp.int16),
            pltpu.VMEM((2, 4, 4, 96, 512), BF16),
            pltpu.VMEM((2, 3, 4, 96, 512), BF16),
            pltpu.VMEM((2, 3, 4, 96, 512), BF16),
            pltpu.VMEM((768, 128), F32),
            pltpu.VMEM((8, 128), F32),
            pltpu.VMEM((8, 8, 128), F32),
            pltpu.VMEM((16, 16, 128), F32),
            pltpu.VMEM((8, 8, 128), F32),
            dma((5,)), dma((NQ, 4)),
            dma((4,)), dma((4, 2)), dma((2, 6)), dma((2, 6)),
            dma((6,)), dma((6,)), dma((4,)), dma((4,)),
            dma((2, 2)), dma((2, 2)), dma((2, 6)), dma((2, 6)), dma((2, 4)), dma((2, 4)),
            dma((NP, 3)), dma((NP, 3)), dma((NP, 3)), dma((NP, 3)), dma((NQ, 3)), dma((NQ, 3)),
            dma((8,)), dma((8,)),
            dma((8,)), dma((8,)), dma((16,)), dma((16,)),
        ],
        compiler_params=pltpu.CompilerParams(
            collective_id=0, has_side_effects=True, vmem_limit_bytes=60 * 1024 * 1024
        ),
    )(sigma_ss, l_cs, g_cc, pattern.T, sup_sizes, owner.reshape(1, 48))
    sel_cs, log_var = pl.pallas_call(
        hand_over,
        out_shape=(jax.ShapeDtypeStruct((768, 512), F32), jax.ShapeDtypeStruct((1, 48), F32)),
        in_specs=[vmem, vmem],
        out_specs=(vmem, vmem),
    )(sel_cs, log_var)
    return (sel_cs, log_var.reshape(48))


def solution(mesh):
    in_specs = (
        P("col", "row"),
        P("row", "col"),
        P("row", "col"),
        P(None, "col"),
        P(),
        P(("row", "col")),
    )
    out_specs = (P("row", "col"), P(("row", "col")))
    return jax.shard_map(
        per_device, mesh=mesh, in_specs=in_specs, out_specs=out_specs, check_vma=False
    )
```

```python
import jax
import jax.numpy as jnp
from jax import lax
from jax.experimental import pallas as pl
from jax.experimental.pallas import tpu as pltpu
from jax.sharding import PartitionSpec as P

NSUP = 16
MESH = pl.DeviceIdType.MESH
F32 = jnp.float32
BF16 = jnp.bfloat16
PASSES = ((0, 0, 32), (0, 32, 64), (1, 0, 96))
PASS_PIECES = ((0,), (1, 2), (3, 4, 5, 6))
PIECES = (
    (0, 0, 32), (0, 32, 32), (0, 64, 32),
    (1, 0, 32), (1, 32, 32), (1, 64, 16), (1, 80, 16),
)
CHUNKS = ((0, 0, 32), (0, 32, 32), (0, 64, 32), (1, 0, 32), (1, 32, 32), (1, 64, 16), (1, 80, 16))
CHUNK_PIECES = ((0,), (1,), (2,), (3,), (4,), (5,), (6,))
ORDER = (
    ("d", 0), ("d", 1), ("c", 0), ("d", 2), ("c", 1), ("d", 3), ("f", 0), ("c", 2), ("d", 4), ("d", 5), ("f", 1), ("c", 3), ("d", 6), ("f", 2), ("c", 4), ("c", 5), ("f", 3), ("c", 6), ("f", 4), ("f", 5), ("f", 6),
)
NP = len(PIECES)
NQ = len(CHUNKS)
FAR_ORDER = (2, 1, 3)


def kernel(
    sigma_ref, l_hbm, g_hbm, pattern_ref, sizes_ref, owner_ref,
    sel_ref, log_ref,
    out_ref, l_ref, g_ref, gt_ref, gbuf, mbuf, sbuf, acc, ysend, yrecv, zc, pbuf, rz, cross, fac_ref, fa, ca, cb,
    local_sem, out_sem, ga_send, ga_recv, gg_send, gg_recv,
    m_send, m_recv, m_sib_send, m_sib_recv,
    sa_send, sa_recv, s_send, s_recv, s_sib_send, s_sib_recv,
    y_send, y_recv, x_send, x_recv, z_send, z_recv,
    fr_send, fr_recv, cr_send, cr_recv, cc_send, cc_recv,
):
    r = lax.axis_index("row")
    c = lax.axis_index("col")
    y, i = r // 2, r % 2
    x, z = c // 4, c % 4
    sib = 2 * y + 1 - i
    t = z // 2
    same = i == t
    other = i != t

    def at_x(d):
        return lax.rem(x + d, 4)

    def at_y(d):
        return lax.rem(y + d, 4)

    def at_z(d):
        return lax.rem(z + d, 4)

    def remote(src, dst, send, recv, row, col):
        return pltpu.make_async_remote_copy(
            src_ref=src, dst_ref=dst, send_sem=send, recv_sem=recv,
            device_id=(row, col), device_id_type=MESH,
        )

    def arrived(dst, recv):
        pltpu.make_async_copy(dst, dst, recv).wait()

    pending = []

    def send(*args):
        copy = remote(*args)
        copy.start()
        pending.append(copy)

    def sent():
        for copy in pending:
            copy.wait_send()
        pending.clear()

    barrier = pltpu.get_barrier_semaphore()
    partners = [(r, lax.rem(c + d, 16)) for d in range(1, 16)]
    partners += [(lax.rem(r + d, 8), c) for d in range(1, 8)]
    partners += [(sib, 4 * at_x(d) + z) for d in range(1, 4)]
    partners += [(sib, 4 * x + at_z(d)) for d in range(1, 4)]
    for partner in partners:
        pl.semaphore_signal(barrier, inc=1, device_id=partner, device_id_type=MESH)
    l_copy = pltpu.make_async_copy(l_hbm, l_ref, local_sem.at[3])
    g_copy_in = pltpu.make_async_copy(g_hbm, g_ref, local_sem.at[4])
    g_copy_in.start()
    l_copy.start()

    ends, total_size = [], jnp.int32(0)
    for s in range(NSUP):
        total_size = total_size + sizes_ref[s]
        ends.append(total_size)
    pattern = pattern_ref[...].astype(F32)
    block_mask = []
    for n in range(6):
        place = jnp.int32(0)
        for s in range(NSUP):
            place = place + (ends[s] <= 6 * r + n).astype(jnp.int32)
        place = jnp.minimum(place, NSUP - 1)
        lane = lax.broadcasted_iota(jnp.int32, (4, NSUP), 1)
        column = jnp.sum(jnp.where(lane == place, pattern, 0.0), axis=1, keepdims=True)
        block_mask.append([column[m:m + 1] for m in range(4)])

    g_copy_in.wait()
    gt_ref[...] = g_ref[...].T.reshape(4, 96, 768)
    wide = g_ref[...].astype(F32)
    squares = jnp.sum(wide * wide, axis=0, keepdims=True)
    fac_ref[...] = jnp.zeros((8, 128), F32)
    for n in range(3):
        fac_ref[n:n + 1] = squares[:, n * 128:(n + 1) * 128]

    l_copy.wait()
    for n in range(6):
        for m in range(4):
            block = l_ref[n * 128:(n + 1) * 128, m * 128:(m + 1) * 128].astype(F32)
            mbuf[i, x, n // 3, (n % 3) * 128:(n % 3 + 1) * 128, m * 128:(m + 1) * 128] = (
                block * block_mask[n][m]
            ).astype(BF16)
    pl.semaphore_wait(barrier, len(partners))

    fa[r] = fac_ref[...]
    for d in range(1, 8):
        send(fac_ref, fa.at[r], fr_send.at[d], fr_recv.at[d], lax.rem(r + d, 8), c)

    def factor_dst():
        return gbuf.at[lax.rem(z, 2), x, i]

    def factor_copies(rel):
        copies = []
        for d in range(0 if rel else 1, 4):
            copies.append(remote(
                gt_ref.at[at_x(d)], factor_dst(), ga_send.at[d], ga_recv.at[d, rel],
                2 * y + t, 4 * at_x(d) + z,
            ))
        return copies

    @pl.when(same)
    def _():
        pltpu.make_async_copy(gt_ref.at[x], factor_dst(), local_sem.at[0]).start()
        for copy in factor_copies(0):
            copy.start()

    @pl.when(other)
    def _():
        for copy in factor_copies(1):
            copy.start()

    def sigma_part(l, half):
        return sigma_ref.at[pl.ds(half * 256, 256), pl.ds(pl.multiple_of(l * 512, 512), 512)]

    def sigma_own():
        return [
            pltpu.make_async_copy(sigma_part(lax.rem(z, 2), h), sbuf.at[y, z, h], local_sem.at[1 + h])
            for h in range(2)
        ]

    def sigma_copy(l):
        return [
            remote(
                sigma_part(l, h), sbuf.at[y, z, h],
                sa_send.at[l, h], sa_recv.at[lax.rem(z, 2), h], 2 * y + t, 4 * x + 2 * i + l,
            )
            for h in range(2)
        ]

    @pl.when(same)
    def _():
        for copy in sigma_own() + sigma_copy(1 - lax.rem(z, 2)):
            copy.start()

    @pl.when(other)
    def _():
        for first, second in zip(sigma_copy(0), sigma_copy(1)):
            first.start()
            second.start()

    def ring_first(src, slot, snd, rcv, right, left, me):
        send(src(0), slot(me, 0), snd.at[0], rcv.at[0], *right)
        send(src(1), slot(me, 1), snd.at[2], rcv.at[2], *left)
        send(src(1), slot(me, 1), snd.at[1], rcv.at[1], *right)
        send(src(0), slot(me, 0), snd.at[3], rcv.at[3], *left)

    def ring_forward(slot, snd, rcv, right, left, at):
        arrived(slot(at(3), 0), rcv.at[0])
        send(slot(at(3), 0), slot(at(3), 0), snd.at[4], rcv.at[4], *right)
        arrived(slot(at(1), 1), rcv.at[2])
        send(slot(at(1), 1), slot(at(1), 1), snd.at[5], rcv.at[5], *left)

    def ring_rest(slot, rcv, at):
        arrived(slot(at(3), 1), rcv.at[1])
        arrived(slot(at(1), 0), rcv.at[3])

    def ring_far(slot, rcv, at):
        arrived(slot(at(2), 0), rcv.at[4])
        arrived(slot(at(2), 1), rcv.at[5])

    x_right, x_left = (r, 4 * at_x(1) + z), (r, 4 * at_x(3) + z)
    y_right, y_left = (2 * at_y(1) + i, c), (2 * at_y(3) + i, c)

    def m_slot(place, half):
        return mbuf.at[i, place, half]

    def m_share(n, place):
        send(mbuf.at[i, place], mbuf.at[i, place], m_sib_send.at[n], m_sib_recv.at[n], sib, c)

    s_block = [jnp.where(same, lax.rem(z, 2), 0)]
    s_block.append(1 - s_block[0])

    def s_slot(order):
        return lambda place, half: sbuf.at[place, 2 * i + s_block[order], half]

    def s_share(order, n, place):
        block = sbuf.at[place, 2 * i + s_block[order]]
        send(block, block, s_sib_send.at[order, n], s_sib_recv.at[order, n], sib, c)

    def s_first(order):
        slot = s_slot(order)
        snd, rcv = s_send.at[order], s_recv.at[order]
        ring_first(lambda h: slot(y, h), slot, snd, rcv, y_right, y_left, y)
        s_share(order, 0, y)

    def s_forward(order):
        ring_forward(s_slot(order), s_send.at[order], s_recv.at[order], y_right, y_left, at_y)

    def s_rest(order):
        ring_rest(s_slot(order), s_recv.at[order], at_y)
        s_share(order, 1, at_y(3))
        s_share(order, 2, at_y(1))

    def s_far(order):
        ring_far(s_slot(order), s_recv.at[order], at_y)
        s_share(order, 3, at_y(2))

    def s_all():
        for order in range(2):
            for n, d in enumerate((0, 3, 1, 2)):
                place = 2 * (1 - i) + sib_block[order]
                arrived(sbuf.at[at_y(d), place], s_sib_recv.at[order, n])

    sib_block = [jnp.where(other, lax.rem(z, 2), 0)]
    sib_block.append(1 - sib_block[0])

    ring_first(lambda h: m_slot(x, h), m_slot, m_send, m_recv, x_right, x_left, x)
    m_share(0, x)

    @pl.when(same)
    def _():
        for copy in sigma_own():
            copy.wait()

    @pl.when(other)
    def _():
        for h in range(2):
            arrived(sbuf.at[y, 2 * i, h], sa_recv.at[0, h])

    s_first(0)

    def g_half(zl, half):
        return gbuf.at[zl, pl.ds(2 * half, 2)]

    def g_copy(zl, half, n, d):
        return remote(
            g_half(zl, half), g_half(zl, half), gg_send.at[zl, n], gg_recv.at[zl, n],
            r, 4 * x + at_z(d),
        )

    def g_source(zl):
        return [g_copy(zl, 0, 0, 1), g_copy(zl, 1, 2, 3), g_copy(zl, 1, 1, 1), g_copy(zl, 0, 3, 3)]

    def g_from(zl):
        return lax.rem(z + 4 - (2 * i + zl), 4)

    @pl.when(same)
    def _():
        pltpu.make_async_copy(gt_ref.at[x], factor_dst(), local_sem.at[0]).wait()
        for d in range(4):
            for rel in range(2):
                if d or rel:
                    src_core = 1 - i if rel else i
                    arrived(gbuf.at[lax.rem(z, 2), at_x(4 - d), src_core], ga_recv.at[d, rel])

    for zl in range(2):
        @pl.when(g_from(zl) == 0)
        def _():
            for copy in g_source(zl):
                copy.start()

    for h in range(2):
        arrived(sbuf.at[y, 2 * i + s_block[1], h], sa_recv.at[s_block[1], h])
    s_first(1)

    def g_forward():
        for zl in range(2):
            @pl.when(g_from(zl) == 1)
            def _():
                arrived(g_half(zl, 0), gg_recv.at[zl, 0])
                g_copy(zl, 0, 4, 1).start()

            @pl.when(g_from(zl) == 3)
            def _():
                arrived(g_half(zl, 1), gg_recv.at[zl, 2])
                g_copy(zl, 1, 5, 3).start()

    def g_rest():
        for zl in range(2):
            @pl.when(g_from(zl) == 1)
            def _():
                arrived(g_half(zl, 1), gg_recv.at[zl, 1])

            @pl.when(g_from(zl) == 3)
            def _():
                arrived(g_half(zl, 0), gg_recv.at[zl, 3])

            @pl.when(g_from(zl) == 2)
            def _():
                arrived(g_half(zl, 0), gg_recv.at[zl, 4])
                arrived(g_half(zl, 1), gg_recv.at[zl, 5])

    def g_sent():
        for zl in range(2):
            @pl.when(g_from(zl) == 0)
            def _():
                for copy in g_source(zl):
                    copy.wait_send()

            @pl.when(g_from(zl) == 1)
            def _():
                g_copy(zl, 0, 4, 1).wait_send()

            @pl.when(g_from(zl) == 3)
            def _():
                g_copy(zl, 1, 5, 3).wait_send()

    s_forward(0)
    g_forward()
    ring_forward(m_slot, m_send, m_recv, x_right, x_left, at_x)
    ring_rest(m_slot, m_recv, at_x)
    m_share(1, at_x(3))
    m_share(2, at_x(1))
    s_rest(0)
    s_forward(1)
    s_rest(1)

    ring_far(m_slot, m_recv, at_x)
    m_share(3, at_x(2))
    g_rest()
    for n, d in enumerate((0, 3, 1, 2)):
        arrived(mbuf.at[1 - i, at_x(d)], m_sib_recv.at[n])

    def zeta_part(q):
        zl, start, rows = PASSES[q]
        here = slice(start, start + rows)
        g0 = gbuf[zl, :, 0, here].reshape(4 * rows, 768)
        g1 = gbuf[zl, :, 1, here].reshape(4 * rows, 768)

        def step(k, carry):
            total = jnp.dot(g0, mbuf[0, k].reshape(768, 512), preferred_element_type=F32)
            total += jnp.dot(g1, mbuf[1, k].reshape(768, 512), preferred_element_type=F32)
            acc[zl, :, k, here] = total.reshape(4, rows, 512)
            return carry

        lax.fori_loop(0, 4, step, 0)

    def zeta_send(q):
        zl, start, rows = PIECES[q]
        here = slice(start, start + rows)
        for d in FAR_ORDER:
            parts = [acc[zl, at_y(d), k, here] for k in range(4)]
            top = jnp.abs(parts[0])
            for part in parts[1:]:
                top = jnp.maximum(top, jnp.abs(part))
            top = jnp.max(top, axis=1, keepdims=True)
            power = jnp.floor(jnp.log2(jnp.maximum(top, 1e-30)) + 1.01)
            up = jnp.exp2(15.0 - power)
            for k in range(4):
                code = jnp.round(parts[k] * up).astype(jnp.int32).astype(jnp.int16)
                ysend[zl, d - 1, here, k * 512:(k + 1) * 512] = code
            ysend[zl, d - 1, here, 2048:] = jnp.broadcast_to(
                power.astype(jnp.int32), (rows, 128)
            ).astype(jnp.int16)
            send(
                ysend.at[zl, d - 1, pl.ds(start, rows)], yrecv.at[zl, d - 1, pl.ds(start, rows)],
                y_send.at[q, d - 1], y_recv.at[q, d - 1], 2 * at_y(d) + i, c,
            )

    def zeta_done(q):
        zl, start, rows = PIECES[q]
        here = slice(start, start + rows)
        for d in range(3):
            arrived(yrecv.at[zl, d, pl.ds(start, rows)], y_recv.at[q, d])
        down = []
        for d in range(3):
            power = yrecv[zl, d, here, 2048:].astype(jnp.int32).astype(F32)
            down.append(jnp.exp2(power - 15.0)[:, 0:1])
        for k in range(4):
            total = acc[zl, y, k, here]
            for d in range(3):
                code = yrecv[zl, d, here, k * 512:(k + 1) * 512]
                total += code.astype(jnp.int32).astype(F32) * down[d]
            zc[zl, k, x, here] = total.astype(BF16)
        block = zc.at[zl, :, x, pl.ds(start, rows)]
        for d in FAR_ORDER:
            send(block, block, x_send.at[q, d - 1], x_recv.at[q, d - 1], r, 4 * at_x(d) + z)

    def product(q, zt):
        zl, start, rows = CHUNKS[q]
        total = None
        for k in range(4):
            part = lax.dot_general(
                zc[zl, k, :, start:start + rows].reshape(4 * rows, 512), sbuf[k, zt].reshape(512, 512),
                (((1,), (1,)), ((), ())), preferred_element_type=F32,
            )
            total = part if total is None else total + part
        return total

    def row_places(q):
        zl, start, rows = CHUNKS[q]
        return [(pl.ds(zl * 384 + p * 96 + start, rows), slice(p * rows, (p + 1) * rows)) for p in range(4)]

    def coupling_part(q):
        zl, start, rows = CHUNKS[q]
        here = pl.ds(start, rows)
        for piece in CHUNK_PIECES[q]:
            _, first, some = PIECES[piece]
            for d in range(1, 4):
                arrived(zc.at[zl, :, at_x(4 - d), pl.ds(first, some)], x_recv.at[piece, d - 1])
        for d in FAR_ORDER:
            pbuf[zl, d - 1, :, start:start + rows] = product(q, at_z(d)).astype(BF16).reshape(4, rows, 512)
            send(
                pbuf.at[zl, d - 1, :, here], rz.at[zl, d - 1, :, here],
                z_send.at[q, d - 1], z_recv.at[q, d - 1], r, 4 * x + at_z(d),
            )
        total = product(q, z)
        for place, part in row_places(q):
            out_ref[place, :] = total[part]

    def out_copy(q, p):
        place = row_places(q)[p][0]
        return pltpu.make_async_copy(out_ref.at[place], sel_ref.at[place], out_sem.at[q, p])

    def coupling_done(q):
        zl, start, rows = CHUNKS[q]
        for d in range(3):
            arrived(rz.at[zl, d, :, pl.ds(start, rows)], z_recv.at[q, d])
        for p, (place, part) in enumerate(row_places(q)):
            total = out_ref[place, :]
            for d in range(3):
                total += rz[zl, d, p, start:start + rows].astype(F32)
            total = -total
            block = (zl * 384 + p * 96 + start) // 128
            out_ref[place, :] = jnp.concatenate(
                [total[:, m * 128:(m + 1) * 128] * block_mask[block][m] for m in range(4)], axis=1
            )
            out_copy(q, p).start()
            terms = total * zc[zl, x, p, start:start + rows].astype(F32)
            cross[place, :] = terms[:, 0:128] + terms[:, 128:256] + terms[:, 256:384] + terms[:, 384:512]

    for n, pieces in enumerate(PASS_PIECES):
        zeta_part(n)
        for piece in pieces:
            zeta_send(piece)
        if n == 0:
            s_far(0)
        if n == 1:
            s_far(1)
    for kind, n in ORDER:
        if (kind, n) == ("c", 0):
            s_all()
        if (kind, n) == ("f", 4):
            for d in range(1, 8):
                arrived(fa.at[lax.rem(r + 8 - d, 8)], fr_recv.at[d])
            ca[c, 8:16] = jnp.sum(fa[...], axis=0)
            ca[c, 0:8] = jnp.zeros((8, 128), F32)
        {"d": zeta_done, "c": coupling_part, "f": coupling_done}[kind](n)

    sums = jnp.sum(cross[...].T, axis=0, keepdims=True)
    for n in range(6):
        ca[c, n:n + 1] = sums[:, n * 128:(n + 1) * 128]
    for d in range(1, 16):
        send(ca.at[c], ca.at[c], cc_send.at[d], cc_recv.at[d], r, lax.rem(c + d, 16))
    @pl.when(same)
    def _():
        for copy in factor_copies(0) + sigma_copy(1 - lax.rem(z, 2)):
            copy.wait_send()

    @pl.when(other)
    def _():
        for copy in factor_copies(1) + sigma_copy(0) + sigma_copy(1):
            copy.wait_send()

    g_sent()
    sent()
    for q in range(NQ):
        for p in range(4):
            out_copy(q, p).wait()
    for d in range(1, 16):
        arrived(ca.at[lax.rem(c + 16 - d, 16)], cc_recv.at[d])
    cb[r] = jnp.sum(ca[:, 0:8], axis=0)
    for d in range(1, 8):
        send(cb.at[r], cb.at[r], cr_send.at[d], cr_recv.at[d], lax.rem(r + d, 8), c)
    wanted = jnp.broadcast_to(owner_ref[...].astype(F32), (128, 48)).T
    lanes = lax.broadcasted_iota(jnp.int32, (48, 128), 1).astype(F32)
    for d in range(1, 8):
        arrived(cb.at[lax.rem(r + 8 - d, 8)], cr_recv.at[d])
    picked = jnp.zeros((48, 128), F32)
    for n in range(48):
        row = jnp.log(ca[n // 3, 8 + n % 3:9 + n % 3] - cb[n // 6, n % 6:n % 6 + 1])
        picked = jnp.where(wanted - float(128 * n) == lanes, row, picked)
    log_ref[...] = jnp.sum(picked.T, axis=0, keepdims=True)

    sent()


def hand_over(from_ref, log_from_ref, to_ref, log_to_ref):
    to_ref[...] = from_ref[...]
    log_to_ref[...] = log_from_ref[...]


def per_device(sigma_ss, l_cs, g_cc, pattern, sup_sizes, owner):
    dma = pltpu.SemaphoreType.DMA
    any_space = pl.BlockSpec(memory_space=pl.ANY)
    vmem = pl.BlockSpec(memory_space=pltpu.VMEM)
    smem = pl.BlockSpec(memory_space=pltpu.SMEM)
    sel_cs, log_var = pl.pallas_call(
        kernel,
        out_shape=(
            jax.ShapeDtypeStruct((768, 512), F32),
            jax.ShapeDtypeStruct((1, 48), F32),
        ),
        in_specs=[any_space, any_space, any_space, vmem, smem, vmem],
        out_specs=(any_space, vmem),
        scratch_shapes=[
            pltpu.VMEM((768, 512), F32),
            pltpu.VMEM((768, 512), BF16),
            pltpu.VMEM((768, 384), BF16),
            pltpu.VMEM((4, 96, 768), BF16),
            pltpu.VMEM((2, 4, 2, 96, 768), BF16),
            pltpu.VMEM((2, 4, 2, 384, 512), BF16),
            pltpu.VMEM((4, 4, 2, 256, 512), BF16),
            pltpu.VMEM((2, 4, 4, 96, 512), F32),
            pltpu.VMEM((2, 3, 96, 2176), jnp.int16),
            pltpu.VMEM((2, 3, 96, 2176), jnp.int16),
            pltpu.VMEM((2, 4, 4, 96, 512), BF16),
            pltpu.VMEM((2, 3, 4, 96, 512), BF16),
            pltpu.VMEM((2, 3, 4, 96, 512), BF16),
            pltpu.VMEM((768, 128), F32),
            pltpu.VMEM((8, 128), F32),
            pltpu.VMEM((8, 8, 128), F32),
            pltpu.VMEM((16, 16, 128), F32),
            pltpu.VMEM((8, 8, 128), F32),
            dma((5,)), dma((NQ, 4)),
            dma((4,)), dma((4, 2)), dma((2, 6)), dma((2, 6)),
            dma((6,)), dma((6,)), dma((4,)), dma((4,)),
            dma((2, 2)), dma((2, 2)), dma((2, 6)), dma((2, 6)), dma((2, 4)), dma((2, 4)),
            dma((NP, 3)), dma((NP, 3)), dma((NP, 3)), dma((NP, 3)), dma((NQ, 3)), dma((NQ, 3)),
            dma((8,)), dma((8,)),
            dma((8,)), dma((8,)), dma((16,)), dma((16,)),
        ],
        compiler_params=pltpu.CompilerParams(
            collective_id=0, has_side_effects=True, vmem_limit_bytes=60 * 1024 * 1024
        ),
    )(sigma_ss, l_cs, g_cc, pattern.T, sup_sizes, owner.reshape(1, 48))
    sel_cs, log_var = pl.pallas_call(
        hand_over,
        out_shape=(jax.ShapeDtypeStruct((768, 512), F32), jax.ShapeDtypeStruct((1, 48), F32)),
        in_specs=[vmem, vmem],
        out_specs=(vmem, vmem),
    )(sel_cs, log_var)
    return (sel_cs, log_var.reshape(48))


def solution(mesh):
    in_specs = (
        P("col", "row"),
        P("row", "col"),
        P("row", "col"),
        P(None, "col"),
        P(),
        P(("row", "col")),
    )
    out_specs = (P("row", "col"), P(("row", "col")))
    return jax.shard_map(
        per_device, mesh=mesh, in_specs=in_specs, out_specs=out_specs, check_vma=False
    )
```
